32 devices in a mesh: grp: 2 (over x), lat: 16 (over z, y, core).
Axes of the slice: x: 2, y: 2, z: 4, core: 2. Of those that a mesh axis runs over, the one named last changes fastest.
Arguments:
- features: bfloat16 [2, 32, 192, 512], P('grp', 'lat'), parts along dimension 0, may hold values from -120 to 120
- noise_index: int32 [2], P('grp'), parts along dimension 0, may hold values from 0 to 17
- sigma_table: float32 [18], replicated, may hold values from 0.002 to 80
- affine_weight: bfloat16 [128, 1024], replicated, may hold values from -0.5 to 0.5
- norm_gain: float32 [3, 512], replicated, may hold values from 0.1 to 1.9
- norm_bias: float32 [3, 512], replicated, may hold values from -3 to 3
- conv1_weight: bfloat16 [3, 3, 512, 512], replicated, may hold values from -0.09375 to 0.09375
- conv2_weight: bfloat16 [3, 3, 512, 512], replicated, may hold values from -0.09375 to 0.09375
- conv_bias: float32 [2, 512], replicated, may hold values from -3 to 3
- qkv_weight: bfloat16 [512, 1536], replicated, may hold values from -3 to 3
- proj_weight: bfloat16 [512, 512], replicated, may hold values from -0.25 to 0.25
- proj_bias: float32 [512], replicated, may hold values from -3 to 3
Outputs:
- bottleneck: bfloat16 [2, 16, 96, 512], P('grp', 'lat'), parts along dimension 0
The draws below stay inside these ranges and needn't reach their ends.
There are 2 independent parts, one for each index of `grp`. The reference program is written for one: setup_inputs(seed, part) draws one part's arguments, and reference() takes and returns one part's arrays. A program takes and returns all parts, laid end to end along the dimension named above; an argument that names none is the same for every part. Nothing has to cross between parts.
All inputs are finite; a program needn't handle non-finite values.
Results may differ from the reference program's by a relative error of at most 0.012.
The reference program's roundings to bfloat16 on the way (of `fourier`, `active`, `middle`, `level_one`, `normed`, `projected`, `weights` and `attended`) count: a program that leaves them out, or rounds other values in their place, can miss the bound.
Values may be sent and summed in bfloat16 or wider, within the bound.
No kernel may reach another device: no remote copies, remote signals or barrier semaphores. Data moves between devices by JAX's collectives and lax.ppermute only.
A program may use at most 128 MiB of HBM per device.

```python
import math
import jax
import jax.numpy as jnp
from jax import lax

C = 512
HEAD_DIM = 64
GROUPS = 32
FREQS = 64
LEVELS = 18
MEMBERS = 1
W1 = 192
H1 = 32


def draw_features(key, part):
    base_key, chan_key, rough_key, row_key = jax.random.split(key, 4)
    full_shape = (MEMBERS, H1, W1, C)
    row_factor = jnp.exp(jax.random.uniform(row_key, (H1,), jnp.float32, 0.0, jnp.log(10.0)))
    channel_scale = jnp.exp(jax.random.uniform(chan_key, (C,), jnp.float32, 0.0, jnp.log(10.0)))
    roughness = jnp.exp(jax.random.uniform(rough_key, (1, H1, W1, 1), jnp.float32, 0.0, jnp.log(2.0)))
    samples = jnp.clip(jax.random.normal(base_key, full_shape, jnp.float32), -6.0, 6.0)
    values = samples * row_factor[None, :, None, None] * channel_scale * roughness / 10.0
    return values.astype(jnp.bfloat16)


def draw_qkv_weight(key, part):
    own_key = jax.random.fold_in(key, 0)
    own_part = jnp.clip(jax.random.normal(own_key, (C, 3 * C), jnp.float32), -6.0, 6.0)
    factor = jnp.concatenate([jnp.full((1, 2 * C), 1.7, jnp.float32), jnp.ones((1, C), jnp.float32)], axis=1)
    table = own_part * factor / C ** 0.5
    return table.astype(jnp.bfloat16)


def gaussian(key, extent, width, most, held_as=jnp.bfloat16):
    array = width * jax.random.normal(key, extent, jnp.float32)
    return jnp.clip(array, min=-most, max=most).astype(held_as)


def setup_inputs(seed: int = 0, part: int = 0) -> dict:
    key_list = jax.random.split(jax.random.key(seed), 13)
    part_keys = jax.random.split(jax.random.fold_in(key_list[12], part), 13)
    return {
        "features": draw_features(jax.random.fold_in(jax.random.fold_in(key_list[12], part), 71), part),
        "noise_index": jax.random.randint(part_keys[1], (MEMBERS,), 0, LEVELS).astype(jnp.int32),
        "sigma_table": jnp.clip(jnp.exp(jax.random.uniform(key_list[2], (LEVELS,), jnp.float32, math.log(0.002), math.log(80.0))), 0.002, 80.0),
        "affine_weight": gaussian(key_list[3], (2 * FREQS, 2 * C), (2 * FREQS) ** -0.5, 0.5),
        "norm_gain": jnp.clip(1.0 + 0.18 * jax.random.normal(key_list[4], (3, C), jnp.float32), 0.1, 1.9),
        "norm_bias": gaussian(key_list[5], (3, C), 0.5, 3.0, jnp.float32),
        "conv1_weight": gaussian(key_list[6], (3, 3, C, C), (9 * C) ** -0.5, 0.09375),
        "conv2_weight": gaussian(key_list[7], (3, 3, C, C), (9 * C) ** -0.5, 0.09375),
        "conv_bias": gaussian(key_list[8], (2, C), 0.5, 3.0, jnp.float32),
        "qkv_weight": draw_qkv_weight(jax.random.fold_in(key_list[12], 71), part),
        "proj_weight": gaussian(key_list[10], (C, C), C ** -0.5, 0.25),
        "proj_bias": gaussian(key_list[11], (C,), 0.5, 3.0, jnp.float32),
    }


eps = 1e-05
skip_gain = 0.7071067811865476

def noise_terms(noise_index, sigma_table, affine_weight):
    levels_count = sigma_table.shape[0]
    chosen = (noise_index[:, None] == jnp.arange(levels_count, dtype=jnp.int32)[None, :]).astype(jnp.float32)
    sigmas = lax.optimization_barrier(jnp.sum(chosen * sigma_table[None, :], axis=1))
    log_level = jnp.log(sigmas) / 4.0
    frequency = jnp.exp(-math.log(10000.0) * jnp.arange(FREQS, dtype=jnp.float32) / FREQS)
    angles = log_level[:, None] * frequency[None, :]
    fourier = jnp.concatenate([jnp.cos(angles), jnp.sin(angles)], axis=1).astype(jnp.bfloat16)
    affine = jnp.dot(fourier, affine_weight, preferred_element_type=jnp.float32)
    channels = affine.shape[1] // 2
    return (affine[:, :channels], affine[:, channels:])

def group_norm(values, norm_scale, norm_offset):
    members, height, breadth, channels = values.shape
    grouped = values.reshape(members, height * breadth, GROUPS, channels // GROUPS)
    center = lax.optimization_barrier(jnp.mean(grouped, axis=(1, 3), keepdims=True))
    spread = lax.optimization_barrier(jnp.mean(jnp.square(grouped - center), axis=(1, 3), keepdims=True))
    normed = (grouped - center) * lax.rsqrt(spread + eps)
    return normed.reshape(values.shape) * norm_scale + norm_offset

def convolve(values, kernel):
    return lax.conv_general_dilated(values.astype(jnp.float32), kernel.astype(jnp.float32), (1, 1), ((1, 1), (1, 1)), dimension_numbers=('NHWC', 'HWIO', 'NHWC'), precision=lax.Precision.HIGHEST)

def attend(query_rows, key_rows, value_rows):
    tokens = query_rows.shape[0]
    blocking = math.gcd(tokens, 512)
    key_full = key_rows.astype(jnp.float32)
    value_full = value_rows.astype(jnp.float32)

    def score_block(query_block):
        scores = jnp.einsum('qhd,khd->qhk', query_block.astype(jnp.float32), key_full, precision=lax.Precision.HIGHEST) * HEAD_DIM ** (-0.5)
        largest = lax.optimization_barrier(jnp.max(scores, axis=-1, keepdims=True))
        weights = jnp.exp(scores - largest)
        totals = lax.optimization_barrier(jnp.sum(weights, axis=-1))
        rounded = lax.optimization_barrier(weights.astype(jnp.bfloat16)).astype(jnp.float32)
        blended = jnp.einsum('qhk,khd->qhd', rounded, value_full, precision=lax.Precision.HIGHEST)
        return blended / totals[..., None]
    blocks = query_rows.reshape(tokens // blocking, blocking, query_rows.shape[1], query_rows.shape[2])
    return lax.map(score_block, blocks).reshape(tokens, -1)

def reference(features, noise_index, sigma_table, affine_weight, norm_gain, norm_bias, conv1_weight, conv2_weight, conv_bias, qkv_weight, proj_weight, proj_bias):
    film_scale, film_shift = noise_terms(noise_index, sigma_table, affine_weight)
    film_scale = film_scale[:, None, None, :]
    film_shift = film_shift[:, None, None, :]
    source = features.astype(jnp.float32)
    active = jax.nn.silu(group_norm(source, norm_gain[0], norm_bias[0])).astype(jnp.bfloat16)
    first_conv = convolve(active, conv1_weight) + conv_bias[0]
    middle = jax.nn.silu(group_norm(first_conv, norm_gain[1], norm_bias[1]) * (1.0 + film_scale) + film_shift).astype(jnp.bfloat16)
    second_conv = convolve(middle, conv2_weight) + conv_bias[1]
    level_one = ((source + second_conv) * skip_gain).astype(jnp.bfloat16)
    level_one = lax.optimization_barrier(level_one)
    members, height, breadth, channels = level_one.shape
    pooled = lax.optimization_barrier(jnp.mean(level_one.astype(jnp.float32).reshape(members, height // 2, 2, breadth // 2, 2, channels), axis=(2, 4)))
    normed = group_norm(pooled, norm_gain[2], norm_bias[2]).astype(jnp.bfloat16)
    tokens = height // 2 * (breadth // 2)
    head_count = channels // HEAD_DIM
    projected = jnp.dot(normed.reshape(members * tokens, channels), qkv_weight, preferred_element_type=jnp.float32).astype(jnp.bfloat16)
    projected = projected.reshape(members, tokens, 3, head_count, HEAD_DIM)
    attended_list = [attend(projected[member, :, 0], projected[member, :, 1], projected[member, :, 2]) for member in range(members)]
    attended = jnp.stack(attended_list).reshape(members * tokens, channels).astype(jnp.bfloat16)
    output_proj = jnp.dot(attended, proj_weight, preferred_element_type=jnp.float32) + proj_bias
    return ((pooled + output_proj.reshape(pooled.shape)) * skip_gain).astype(jnp.bfloat16)
```

```python
import functools
import math

import jax
import jax.numpy as jnp
from jax import lax
from jax.experimental import pallas as pl
from jax.experimental.pallas import tpu as pltpu
from jax.sharding import PartitionSpec as P

HEAD_DIM = 64
GROUPS = 32
FREQS = 64


eps = 1e-05
skip_gain = 0.7071067811865476


def noise_terms(noise_index, sigma_table, affine_weight):
    levels_count = sigma_table.shape[0]
    chosen = (noise_index[:, None] == jnp.arange(levels_count, dtype=jnp.int32)[None, :]).astype(
        jnp.float32
    )
    sigmas = jnp.sum(chosen * sigma_table[None, :], axis=1)
    log_level = jnp.log(sigmas) / 4.0
    frequency = jnp.exp(-math.log(10000.0) * jnp.arange(FREQS, dtype=jnp.float32) / FREQS)
    angles = log_level[:, None] * frequency[None, :]
    fourier = jnp.concatenate([jnp.cos(angles), jnp.sin(angles)], axis=1).astype(jnp.bfloat16)
    affine = jnp.dot(fourier, affine_weight, preferred_element_type=jnp.float32)
    channels = affine.shape[1] // 2
    return (affine[:, :channels], affine[:, channels:])


def shared_sum(vector):
    count = lax.axis_size("lat")
    sent = jnp.broadcast_to(vector[None, None, :], (count, 1, vector.shape[0]))
    return jnp.sum(lax.all_to_all(sent, "lat", 0, 0), axis=(0, 1))


def band_moments(values):
    members, height, breadth, channels = values.shape
    group_width = channels // GROUPS
    entries = height * breadth * group_width * lax.axis_size("lat")
    sums = jnp.sum(values, axis=(0, 1, 2)).reshape(GROUPS, group_width).sum(axis=1)
    squares = jnp.sum(jnp.square(values), axis=(0, 1, 2)).reshape(GROUPS, group_width).sum(axis=1)
    totals = shared_sum(jnp.concatenate([sums, squares, jnp.zeros((128 - 2 * GROUPS,), jnp.float32)]))
    center = totals[:GROUPS] / entries
    spread = totals[GROUPS : 2 * GROUPS] / entries - center * center
    return (center, spread)


def normalize(values, center, spread, norm_scale, norm_offset):
    group_width = values.shape[-1] // GROUPS
    center_full = jnp.repeat(center, group_width)
    factor_full = jnp.repeat(lax.rsqrt(spread + eps), group_width)
    return (values - center_full) * (factor_full * norm_scale) + norm_offset


def convolve(values, kernel):
    return lax.conv_general_dilated(
        values,
        kernel,
        (1, 1),
        ((0, 0), (1, 1)),
        dimension_numbers=("NHWC", "HWIO", "NHWC"),
        preferred_element_type=jnp.float32,
    )


def exchange(block, stride):
    count = lax.axis_size("lat")
    return lax.ppermute(block, "lat", [(i, i ^ stride) for i in range(count)])


def gather_blocks(block):
    count = lax.axis_size("lat")
    slow = [block] + [exchange(block, stride) for stride in range(4, count, 4)]
    wide = slow + [exchange(each, 2) for each in slow]
    return wide + [exchange(each, 1) for each in wide]


def group_total(rows):
    width = rows.shape[1]
    lane = lax.broadcasted_iota(jnp.int32, rows.shape, 1)
    step = 1
    while step < width // GROUPS:
        below = pltpu.roll(rows, step, 1)
        above = pltpu.roll(rows, width - step, 1)
        rows = rows + jnp.where((lane & step) != 0, below, above)
        step *= 2
    return rows


def attention_kernel(count, *refs):
    blocks = refs[:count]
    pooled, norm_gain, norm_bias, qkv_weight, proj_weight, proj_bias, out, keys, values = refs[count:]
    tokens, channels = pooled.shape
    group_width = channels // GROUPS
    sums = jnp.zeros((8, channels), jnp.float32)
    squares = jnp.zeros((8, channels), jnp.float32)
    for block in blocks:
        entry = block[...].astype(jnp.float32).reshape(tokens // 8, 8, channels)
        sums = sums + jnp.sum(entry, axis=0)
        squares = squares + jnp.sum(entry * entry, axis=0)
    sums = jnp.sum(sums, axis=0, keepdims=True)
    squares = jnp.sum(squares, axis=0, keepdims=True)
    row = lax.broadcasted_iota(jnp.int32, (8, channels), 0)
    moments = group_total(jnp.where(row == 0, sums, squares)) / (count * tokens * group_width)
    center = moments[0:1]
    spread = moments[1:2] - center * center
    factor = lax.rsqrt(spread + eps) * norm_gain[...]
    offset = norm_bias[...]

    def normed(entry):
        return ((entry.astype(jnp.float32) - center) * factor + offset).astype(jnp.bfloat16)

    for i, block in enumerate(blocks):
        projected = jnp.dot(
            normed(block[...]), qkv_weight[:, channels:], preferred_element_type=jnp.float32
        ).astype(jnp.bfloat16)
        keys[i * tokens : (i + 1) * tokens, :] = projected[:, :channels]
        values[i * tokens : (i + 1) * tokens, :] = projected[:, channels:]
    queries = jnp.dot(
        normed(pooled[...]), qkv_weight[:, :channels], preferred_element_type=jnp.float32
    ).astype(jnp.bfloat16) * jnp.bfloat16(HEAD_DIM ** (-0.5))
    first = lax.broadcasted_iota(jnp.int32, (tokens, 2 * HEAD_DIM), 1) < HEAD_DIM
    attended = []
    for start in range(0, channels, 2 * HEAD_DIM):
        pair = slice(start, start + 2 * HEAD_DIM)
        query = queries[:, pair]
        zero = jnp.zeros_like(query)
        both = jnp.concatenate([jnp.where(first, query, zero), jnp.where(first, zero, query)], axis=0)
        scores = lax.dot_general(
            both, keys[:, pair], (((1,), (1,)), ((), ())), preferred_element_type=jnp.float32
        )
        weights = jnp.exp(scores - jnp.max(scores, axis=1, keepdims=True))
        totals = jnp.sum(weights, axis=1, keepdims=True)
        blended = (
            jnp.dot(weights.astype(jnp.bfloat16), values[:, pair], preferred_element_type=jnp.float32)
            / totals
        )
        attended.append(jnp.where(first, blended[:tokens], blended[tokens:]).astype(jnp.bfloat16))
    projected = jnp.dot(
        jnp.concatenate(attended, axis=1), proj_weight[...], preferred_element_type=jnp.float32
    )
    out[...] = ((pooled[...] + projected + proj_bias[...]) * skip_gain).astype(jnp.bfloat16)


def attention(blocks, pooled, norm_gain, norm_bias, qkv_weight, proj_weight, proj_bias):
    tokens, channels = pooled.shape
    count = len(blocks)
    return pl.pallas_call(
        functools.partial(attention_kernel, count),
        out_shape=jax.ShapeDtypeStruct((tokens, channels), jnp.bfloat16),
        scratch_shapes=[
            pltpu.VMEM((count * tokens, channels), jnp.bfloat16),
            pltpu.VMEM((count * tokens, channels), jnp.bfloat16),
        ],
        compiler_params=pltpu.CompilerParams(vmem_limit_bytes=48 * 1024 * 1024),
    )(
        *blocks,
        pooled,
        norm_gain.reshape(1, channels),
        norm_bias.reshape(1, channels),
        qkv_weight,
        proj_weight,
        proj_bias.reshape(1, channels),
    )


def local(
    features,
    noise_index,
    sigma_table,
    affine_weight,
    norm_gain,
    norm_bias,
    conv1_weight,
    conv2_weight,
    conv_bias,
    qkv_weight,
    proj_weight,
    proj_bias,
):
    members, height, breadth, channels = features.shape
    count = lax.axis_size("lat")
    place = lax.axis_index("lat")
    below = lax.ppermute(features[:, -2:], "lat", [(i, i + 1) for i in range(count - 1)])
    above = lax.ppermute(features[:, :2], "lat", [(i + 1, i) for i in range(count - 1)])
    film_scale, film_shift = noise_terms(noise_index, sigma_table, affine_weight)
    source = features.astype(jnp.float32)
    center, spread = band_moments(source)

    def inside(rows):
        first = place * height - (rows - height) // 2
        row = first + jnp.arange(rows)
        return ((row >= 0) & (row < count * height))[None, :, None, None]

    wide = jnp.concatenate([below, features, above], axis=1).astype(jnp.float32)
    active = jax.nn.silu(normalize(wide, center, spread, norm_gain[0], norm_bias[0]))
    active = jnp.where(inside(height + 4), active, 0.0).astype(jnp.bfloat16)
    first_conv = convolve(active, conv1_weight) + conv_bias[0]
    center, spread = band_moments(first_conv[:, 1:-1])
    middle = jax.nn.silu(
        normalize(first_conv, center, spread, norm_gain[1], norm_bias[1]) * (1.0 + film_scale[0])
        + film_shift[0]
    )
    middle = jnp.where(inside(height + 2), middle, 0.0).astype(jnp.bfloat16)
    second_conv = convolve(middle, conv2_weight)
    level_one = ((source + second_conv + conv_bias[1]) * skip_gain).astype(jnp.bfloat16)
    level_one = lax.optimization_barrier(level_one)
    low_rows = height // 2
    breadth_low = breadth // 2
    pooled = jnp.mean(
        level_one.astype(jnp.float32).reshape(members, low_rows, 2, breadth_low, 2, channels),
        axis=(2, 4),
    ).reshape(low_rows * breadth_low, channels)
    blocks = gather_blocks(pooled.astype(jnp.bfloat16))
    out = attention(blocks, pooled, norm_gain[2], norm_bias[2], qkv_weight, proj_weight, proj_bias)
    return out.reshape(members, low_rows, breadth_low, channels)


def solution(mesh):
    return jax.shard_map(
        local,
        mesh=mesh,
        in_specs=(
            P("grp", "lat", None, None),
            P("grp"),
            P(),
            P(),
            P(),
            P(),
            P(),
            P(),
            P(),
            P(),
            P(),
            P(),
        ),
        out_specs=P("grp", "lat", None, None),
        check_vma=False,
    )
```

```python
import functools
import math

import jax
import jax.numpy as jnp
from jax import lax
from jax.experimental import pallas as pl
from jax.experimental.pallas import tpu as pltpu
from jax.sharding import PartitionSpec as P

HEAD_DIM = 64
GROUPS = 32
FREQS = 64
GROUP_WIDTH = 16
LANES = 128


eps = 1e-05
skip_gain = 0.7071067811865476


def noise_terms(noise_index, sigma_table, affine_weight):
    levels_count = sigma_table.shape[0]
    chosen = (noise_index[:, None] == jnp.arange(levels_count, dtype=jnp.int32)[None, :]).astype(
        jnp.float32
    )
    sigmas = jnp.sum(chosen * sigma_table[None, :], axis=1)
    log_level = jnp.log(sigmas) / 4.0
    frequency = jnp.exp(-math.log(10000.0) * jnp.arange(FREQS, dtype=jnp.float32) / FREQS)
    angles = log_level[:, None] * frequency[None, :]
    fourier = jnp.concatenate([jnp.cos(angles), jnp.sin(angles)], axis=1).astype(jnp.bfloat16)
    return jnp.dot(fourier, affine_weight, preferred_element_type=jnp.float32)


def group_total(rows):
    width = rows.shape[1]
    lane = lax.broadcasted_iota(jnp.int32, rows.shape, 1)
    step = 1
    while step < GROUP_WIDTH:
        below = pltpu.roll(rows, step, 1)
        above = pltpu.roll(rows, width - step, 1)
        rows = rows + jnp.where((lane & step) != 0, below, above)
        step *= 2
    return rows


def packed_moments(sums, squares):
    channels = sums.shape[1]
    row = lax.broadcasted_iota(jnp.int32, (8, channels), 0)
    totals = group_total(jnp.where(row == 0, sums, squares))
    slot = lax.broadcasted_iota(jnp.int32, (1, LANES), 1) % GROUP_WIDTH
    packed = jnp.zeros((1, LANES), jnp.float32)
    for tile in range(channels // LANES):
        for kind in range(2):
            part = totals[kind : kind + 1, tile * LANES : (tile + 1) * LANES]
            packed = jnp.where(slot == 2 * tile + kind, part, packed)
    return packed


def unpacked_moments(shared, entries, channels):
    packed = jnp.sum(shared, axis=0, keepdims=True)
    row = lax.broadcasted_iota(jnp.int32, (8, LANES), 0)
    slot = lax.broadcasted_iota(jnp.int32, (8, LANES), 1) % GROUP_WIDTH
    totals = group_total(jnp.where(row == slot, packed, 0.0)) / entries
    tiles = channels // LANES
    center = jnp.concatenate([totals[2 * tile : 2 * tile + 1] for tile in range(tiles)], axis=1)
    second = jnp.concatenate([totals[2 * tile + 1 : 2 * tile + 2] for tile in range(tiles)], axis=1)
    return center, second - center * center


def column_sums(values):
    rows, channels = values.shape
    folded = values.reshape(rows // 8, 8, channels)
    sums = jnp.sum(folded, axis=0)
    squares = jnp.sum(folded * folded, axis=0)
    return jnp.sum(sums, axis=0, keepdims=True), jnp.sum(squares, axis=0, keepdims=True)


def silu(values):
    return values / (1.0 + jnp.exp(-values))


def shared(rows):
    count, lanes = rows.shape
    return lax.all_to_all(rows.reshape(count, 1, lanes), "lat", 0, 0).reshape(count, lanes)


def moments_kernel(features, out):
    sums, squares = column_sums(features[...].astype(jnp.float32))
    out[...] = jnp.broadcast_to(packed_moments(sums, squares), out.shape)


def moments(features):
    return pl.pallas_call(
        moments_kernel,
        out_shape=jax.ShapeDtypeStruct((lax.axis_size("lat"), LANES), jnp.float32),
    )(features)


def shifted(line, breadth, lines, spread):
    channels = line.shape[1]
    lines[8 : 8 + breadth, :] = line
    spread[:, channels : 2 * channels] = line.astype(jnp.bfloat16)
    spread[:, :channels] = lines[7 : 7 + breadth, :].astype(jnp.bfloat16)
    spread[:, 2 * channels :] = lines[9 : 9 + breadth, :].astype(jnp.bfloat16)


def convolved(spread, weight, copies, first, rows, breadth):
    total = None
    for tap in range(3):
        copies[tap].wait()
        patch = spread[(first + tap) * breadth : (first + tap + rows) * breadth, :]
        part = jnp.dot(patch, weight[tap], preferred_element_type=jnp.float32)
        total = part if total is None else total + part
    return total


def weight_copies(source, weight, sems):
    copies = [pltpu.make_async_copy(source.at[tap], weight.at[tap], sems.at[tap]) for tap in range(3)]
    for each in copies:
        each.start()
    return copies


def first_kernel(
    height, breadth, below, own, above, sums, gain, bias, weight_hbm, conv_bias, out, packed, spread, lines, weight, sems
):
    count = lax.axis_size("lat")
    place = lax.axis_index("lat")
    channels = own.shape[1]
    copies = weight_copies(weight_hbm, weight, sems)
    lines[...] = jnp.zeros_like(lines)
    center, variance = unpacked_moments(
        sums[...], count * height * breadth * (channels // GROUPS), channels
    )
    factor = lax.rsqrt(variance + eps) * gain[...]
    offset = bias[...]
    for row in range(height + 4):
        near = row - 2
        if near < 0:
            block, at = below, near + 2
        elif near < height:
            block, at = own, near
        else:
            block, at = above, near - height
        values = block[at * breadth : (at + 1) * breadth, :].astype(jnp.float32)
        values = silu((values - center) * factor + offset)
        if near < 0:
            values = jnp.where(place > 0, values, 0.0)
        elif near >= height:
            values = jnp.where(place < count - 1, values, 0.0)
        shifted(values, breadth, lines, spread.at[row * breadth : (row + 1) * breadth, :])
    result = convolved(spread, weight, copies, 0, height + 2, breadth) + conv_bias[...]
    out[...] = result
    total, squares = column_sums(result[breadth : (1 + height) * breadth])
    packed[...] = jnp.broadcast_to(packed_moments(total, squares), packed.shape)


def first_convolution(height, breadth, below, own, above, sums, gain, bias, weight, conv_bias):
    channels = own.shape[1]
    count = sums.shape[0]
    plain = pl.BlockSpec(memory_space=pltpu.VMEM)
    return pl.pallas_call(
        functools.partial(first_kernel, height, breadth),
        in_specs=[plain] * 6 + [pl.BlockSpec(memory_space=pl.ANY), plain],
        out_shape=(
            jax.ShapeDtypeStruct(((height + 2) * breadth, channels), jnp.float32),
            jax.ShapeDtypeStruct((count, LANES), jnp.float32),
        ),
        scratch_shapes=[
            pltpu.VMEM(((height + 4) * breadth, 3 * channels), jnp.bfloat16),
            pltpu.VMEM((breadth + 16, channels), jnp.float32),
            pltpu.VMEM((3, 3 * channels, channels), jnp.bfloat16),
            pltpu.SemaphoreType.DMA((3,)),
        ],
        compiler_params=pltpu.CompilerParams(vmem_limit_bytes=40 * 1024 * 1024),
    )(below, own, above, sums, gain, bias, weight.reshape(3, 3 * channels, channels), conv_bias)


def second_kernel(
    height, breadth, first, own, sums, gain, bias, film, weight_hbm, conv_bias, pooled, sent, spread, lines, pairs, weight, sems
):
    count = lax.axis_size("lat")
    place = lax.axis_index("lat")
    channels = own.shape[1]
    copies = weight_copies(weight_hbm, weight, sems)
    lines[...] = jnp.zeros_like(lines)
    center, variance = unpacked_moments(
        sums[...], count * height * breadth * (channels // GROUPS), channels
    )
    factor = lax.rsqrt(variance + eps) * gain[...]
    offset = bias[...]
    scale = 1.0 + film[:, :channels]
    shift = film[:, channels:]
    for row in range(height + 2):
        values = first[row * breadth : (row + 1) * breadth, :]
        values = silu(((values - center) * factor + offset) * scale + shift)
        if row == 0:
            values = jnp.where(place > 0, values, 0.0)
        elif row == height + 1:
            values = jnp.where(place < count - 1, values, 0.0)
        shifted(values, breadth, lines, spread.at[row * breadth : (row + 1) * breadth, :])
    result = convolved(spread, weight, copies, 0, height, breadth)
    level = ((own[...].astype(jnp.float32) + result + conv_bias[...]) * skip_gain).astype(jnp.bfloat16)
    level = level.astype(jnp.float32)
    half = breadth // 2
    for row in range(height // 2):
        start = 2 * row * breadth
        both = level[start : start + breadth] + level[start + breadth : start + 2 * breadth]
        for tile in range(channels // LANES):
            lanes = slice(tile * LANES, (tile + 1) * LANES)
            pairs[...] = both[:, lanes]
            mean = (pairs[pl.ds(0, half, stride=2), :] + pairs[pl.ds(1, half, stride=2), :]) * 0.25
            pooled[row * half : (row + 1) * half, lanes] = mean
            sent[row * half : (row + 1) * half, lanes] = mean.astype(jnp.bfloat16)


def second_convolution(height, breadth, first, own, sums, gain, bias, film, weight, conv_bias):
    channels = own.shape[1]
    tokens = (height // 2) * (breadth // 2)
    plain = pl.BlockSpec(memory_space=pltpu.VMEM)
    return pl.pallas_call(
        functools.partial(second_kernel, height, breadth),
        in_specs=[plain] * 6 + [pl.BlockSpec(memory_space=pl.ANY), plain],
        out_shape=(
            jax.ShapeDtypeStruct((tokens, channels), jnp.float32),
            jax.ShapeDtypeStruct((tokens, channels), jnp.bfloat16),
        ),
        scratch_shapes=[
            pltpu.VMEM(((height + 2) * breadth, 3 * channels), jnp.bfloat16),
            pltpu.VMEM((breadth + 16, channels), jnp.float32),
            pltpu.VMEM((breadth, LANES), jnp.float32),
            pltpu.VMEM((3, 3 * channels, channels), jnp.bfloat16),
            pltpu.SemaphoreType.DMA((3,)),
        ],
        compiler_params=pltpu.CompilerParams(vmem_limit_bytes=40 * 1024 * 1024),
    )(first, own, sums, gain, bias, film, weight.reshape(3, 3 * channels, channels), conv_bias)


def exchange(block, stride):
    count = lax.axis_size("lat")
    return lax.ppermute(block, "lat", [(i, i ^ stride) for i in range(count)])


def gather_blocks(block):
    count = lax.axis_size("lat")
    slow = [block] + [exchange(block, stride) for stride in range(4, count, 4)]
    wide = slow + [exchange(each, 2) for each in slow]
    return wide + [exchange(each, 1) for each in wide]


def attention_kernel(count, *refs):
    blocks = refs[:count]
    pooled, norm_gain, norm_bias, qkv_weight, proj_weight, proj_bias, out, keys, values = refs[count:]
    tokens, channels = pooled.shape
    group_width = channels // GROUPS
    sums = jnp.zeros((8, channels), jnp.float32)
    squares = jnp.zeros((8, channels), jnp.float32)
    for block in blocks:
        entry = block[...].astype(jnp.float32).reshape(tokens // 8, 8, channels)
        sums = sums + jnp.sum(entry, axis=0)
        squares = squares + jnp.sum(entry * entry, axis=0)
    sums = jnp.sum(sums, axis=0, keepdims=True)
    squares = jnp.sum(squares, axis=0, keepdims=True)
    row = lax.broadcasted_iota(jnp.int32, (8, channels), 0)
    moments = group_total(jnp.where(row == 0, sums, squares)) / (count * tokens * group_width)
    center = moments[0:1]
    spread = moments[1:2] - center * center
    factor = lax.rsqrt(spread + eps) * norm_gain[...]
    offset = norm_bias[...]

    def normed(entry):
        return ((entry.astype(jnp.float32) - center) * factor + offset).astype(jnp.bfloat16)

    for i, block in enumerate(blocks):
        projected = jnp.dot(
            normed(block[...]), qkv_weight[:, channels:], preferred_element_type=jnp.float32
        ).astype(jnp.bfloat16)
        keys[i * tokens : (i + 1) * tokens, :] = projected[:, :channels]
        values[i * tokens : (i + 1) * tokens, :] = projected[:, channels:]
    queries = jnp.dot(
        normed(pooled[...]), qkv_weight[:, :channels], preferred_element_type=jnp.float32
    ).astype(jnp.bfloat16) * jnp.bfloat16(HEAD_DIM ** (-0.5))
    first = lax.broadcasted_iota(jnp.int32, (tokens, 2 * HEAD_DIM), 1) < HEAD_DIM
    attended = []
    for start in range(0, channels, 2 * HEAD_DIM):
        pair = slice(start, start + 2 * HEAD_DIM)
        query = queries[:, pair]
        zero = jnp.zeros_like(query)
        both = jnp.concatenate([jnp.where(first, query, zero), jnp.where(first, zero, query)], axis=0)
        scores = lax.dot_general(
            both, keys[:, pair], (((1,), (1,)), ((), ())), preferred_element_type=jnp.float32
        )
        weights = jnp.exp(scores - jnp.max(scores, axis=1, keepdims=True))
        totals = jnp.sum(weights, axis=1, keepdims=True)
        blended = (
            jnp.dot(weights.astype(jnp.bfloat16), values[:, pair], preferred_element_type=jnp.float32)
            / totals
        )
        attended.append(jnp.where(first, blended[:tokens], blended[tokens:]).astype(jnp.bfloat16))
    projected = jnp.dot(
        jnp.concatenate(attended, axis=1), proj_weight[...], preferred_element_type=jnp.float32
    )
    out[...] = ((pooled[...] + projected + proj_bias[...]) * skip_gain).astype(jnp.bfloat16)


def attention(blocks, pooled, norm_gain, norm_bias, qkv_weight, proj_weight, proj_bias):
    tokens, channels = pooled.shape
    count = len(blocks)
    return pl.pallas_call(
        functools.partial(attention_kernel, count),
        out_shape=jax.ShapeDtypeStruct((tokens, channels), jnp.bfloat16),
        scratch_shapes=[
            pltpu.VMEM((count * tokens, channels), jnp.bfloat16),
            pltpu.VMEM((count * tokens, channels), jnp.bfloat16),
        ],
        compiler_params=pltpu.CompilerParams(vmem_limit_bytes=48 * 1024 * 1024),
    )(
        *blocks,
        pooled,
        norm_gain.reshape(1, channels),
        norm_bias.reshape(1, channels),
        qkv_weight,
        proj_weight,
        proj_bias.reshape(1, channels),
    )


def local(
    features,
    noise_index,
    sigma_table,
    affine_weight,
    norm_gain,
    norm_bias,
    conv1_weight,
    conv2_weight,
    conv_bias,
    qkv_weight,
    proj_weight,
    proj_bias,
):
    members, height, breadth, channels = features.shape
    count = lax.axis_size("lat")
    below = lax.ppermute(features[:, -2:], "lat", [(i, i + 1) for i in range(count - 1)])
    above = lax.ppermute(features[:, :2], "lat", [(i + 1, i) for i in range(count - 1)])
    film = noise_terms(noise_index, sigma_table, affine_weight)
    own = features.reshape(height * breadth, channels)
    below = below.reshape(2 * breadth, channels)
    above = above.reshape(2 * breadth, channels)
    sums = shared(moments(own))
    first, packed = first_convolution(
        height, breadth, below, own, above, sums, norm_gain[0:1], norm_bias[0:1], conv1_weight, conv_bias[0:1]
    )
    sums = shared(packed)
    pooled, sent = second_convolution(
        height, breadth, first, own, sums, norm_gain[1:2], norm_bias[1:2], film, conv2_weight, conv_bias[1:2]
    )
    blocks = gather_blocks(sent)
    out = attention(blocks, pooled, norm_gain[2], norm_bias[2], qkv_weight, proj_weight, proj_bias)
    return out.reshape(members, height // 2, breadth // 2, channels)


def solution(mesh):
    return jax.shard_map(
        local,
        mesh=mesh,
        in_specs=(
            P("grp", "lat", None, None),
            P("grp"),
            P(),
            P(),
            P(),
            P(),
            P(),
            P(),
            P(),
            P(),
            P(),
            P(),
        ),
        out_specs=P("grp", "lat", None, None),
        check_vma=False,
    )
```

```python
import functools
import math

import jax
import jax.numpy as jnp
from jax import lax
from jax.experimental import pallas as pl
from jax.experimental.pallas import tpu as pltpu
from jax.sharding import PartitionSpec as P

HEAD_DIM = 64
GROUPS = 32
FREQS = 64
GROUP_WIDTH = 16
LANES = 128
GAIN, BIAS, CONV_BIAS, PROJ_BIAS = 0, 3, 6, 8
VMEM_BYTES = 52 * 1024 * 1024
FAR = pl.BlockSpec(memory_space=pltpu.HBM)
NEAR = pl.BlockSpec(memory_space=pltpu.VMEM)


eps = 1e-05
skip_gain = 0.7071067811865476


def noise_terms(noise_index, sigma_table, affine_weight):
    levels_count = sigma_table.shape[0]
    chosen = (noise_index[:, None] == jnp.arange(levels_count, dtype=jnp.int32)[None, :]).astype(
        jnp.float32
    )
    sigmas = jnp.sum(chosen * sigma_table[None, :], axis=1)
    log_level = jnp.log(sigmas) / 4.0
    frequency = jnp.exp(-math.log(10000.0) * jnp.arange(FREQS, dtype=jnp.float32) / FREQS)
    angles = log_level[:, None] * frequency[None, :]
    fourier = jnp.concatenate([jnp.cos(angles), jnp.sin(angles)], axis=1).astype(jnp.bfloat16)
    return jnp.dot(fourier, affine_weight, preferred_element_type=jnp.float32)


def group_total(rows):
    width = rows.shape[1]
    lane = lax.broadcasted_iota(jnp.int32, rows.shape, 1)
    step = 1
    while step < GROUP_WIDTH:
        below = pltpu.roll(rows, step, 1)
        above = pltpu.roll(rows, width - step, 1)
        rows = rows + jnp.where((lane & step) != 0, below, above)
        step *= 2
    return rows


def packed_moments(sums, squares):
    channels = sums.shape[1]
    row = lax.broadcasted_iota(jnp.int32, (8, channels), 0)
    totals = group_total(jnp.where(row == 0, sums, squares))
    slot = lax.broadcasted_iota(jnp.int32, (1, LANES), 1) % GROUP_WIDTH
    packed = jnp.zeros((1, LANES), jnp.float32)
    for tile in range(channels // LANES):
        for kind in range(2):
            part = totals[kind : kind + 1, tile * LANES : (tile + 1) * LANES]
            packed = jnp.where(slot == 2 * tile + kind, part, packed)
    return packed


def unpacked_moments(shared, entries, channels):
    packed = jnp.sum(shared, axis=0, keepdims=True)
    row = lax.broadcasted_iota(jnp.int32, (8, LANES), 0)
    slot = lax.broadcasted_iota(jnp.int32, (8, LANES), 1) % GROUP_WIDTH
    totals = group_total(jnp.where(row == slot, packed, 0.0)) / entries
    tiles = channels // LANES
    center = jnp.concatenate([totals[2 * tile : 2 * tile + 1] for tile in range(tiles)], axis=1)
    second = jnp.concatenate([totals[2 * tile + 1 : 2 * tile + 2] for tile in range(tiles)], axis=1)
    return center, second - center * center


def column_sums(values):
    rows, channels = values.shape
    folded = values.reshape(rows // 8, 8, channels)
    sums = jnp.sum(folded, axis=0)
    squares = jnp.sum(folded * folded, axis=0)
    return jnp.sum(sums, axis=0, keepdims=True), jnp.sum(squares, axis=0, keepdims=True)


def silu(values):
    return values / (1.0 + jnp.exp(-values))


def shared(rows):
    count, lanes = rows.shape
    return lax.all_to_all(rows.reshape(count, 1, lanes), "lat", 0, 0).reshape(count, lanes)


def fetched(pairs, sems):
    copies = [pltpu.make_async_copy(source, target, sems.at[i]) for i, (source, target) in enumerate(pairs)]
    for each in copies:
        each.start()
    return copies


def moments_kernel(parts, features, out, held, sems):
    rows = features.shape[0] // parts
    spans = [pl.ds(part * rows, rows) for part in range(parts)]
    copies = fetched([(features.at[span], held.at[span]) for span in spans], sems)
    sums, squares = 0.0, 0.0
    for part, copy in enumerate(copies):
        copy.wait()
        more = column_sums(held[part * rows : (part + 1) * rows, :].astype(jnp.float32))
        sums, squares = sums + more[0], squares + more[1]
    out[...] = jnp.broadcast_to(packed_moments(sums, squares), out.shape)


def moments(features):
    parts = 4
    return pl.pallas_call(
        functools.partial(moments_kernel, parts),
        in_specs=[FAR],
        out_shape=(
            jax.ShapeDtypeStruct((lax.axis_size("lat"), LANES), jnp.float32),
            jax.ShapeDtypeStruct(features.shape, features.dtype),
        ),
        scratch_shapes=[pltpu.SemaphoreType.DMA((parts,))],
        compiler_params=pltpu.CompilerParams(vmem_limit_bytes=VMEM_BYTES),
    )(features)


def shifted(line, breadth, lines, spread):
    channels = line.shape[1]
    lines[8 : 8 + breadth, :] = line
    spread[:, channels : 2 * channels] = line.astype(jnp.bfloat16)
    spread[:, :channels] = lines[7 : 7 + breadth, :].astype(jnp.bfloat16)
    spread[:, 2 * channels :] = lines[9 : 9 + breadth, :].astype(jnp.bfloat16)


def convolved(spread, weight, copies, rows, breadth):
    total = None
    for tap, copy in enumerate(copies):
        copy.wait()
        patch = spread[tap * breadth : (tap + rows) * breadth, :]
        part = jnp.dot(patch, weight[tap], preferred_element_type=jnp.float32)
        total = part if total is None else total + part
    return total


def first_kernel(
    height, breadth, below, own, above, sums, table, taps, out, packed, weight, spread, lines, result, sems
):
    count = lax.axis_size("lat")
    place = lax.axis_index("lat")
    channels = own.shape[1]
    copies = fetched([(taps.at[tap], weight.at[tap]) for tap in range(3)], sems)
    lines[...] = jnp.zeros_like(lines)
    center, variance = unpacked_moments(
        sums[...], count * height * breadth * (channels // GROUPS), channels
    )
    factor = lax.rsqrt(variance + eps) * table[GAIN : GAIN + 1]
    offset = table[BIAS : BIAS + 1]
    for row in range(height + 4):
        if row < 2:
            values = below[row * breadth : (row + 1) * breadth, :]
        elif row < height + 2:
            values = own[(row - 2) * breadth : (row - 1) * breadth, :]
        else:
            values = above[(row - height - 2) * breadth : (row - height - 1) * breadth, :]
        values = values.astype(jnp.float32)
        values = silu((values - center) * factor + offset)
        if row < 2:
            values = jnp.where(place > 0, values, 0.0)
        elif row >= height + 2:
            values = jnp.where(place < count - 1, values, 0.0)
        shifted(values, breadth, lines, spread.at[row * breadth : (row + 1) * breadth, :])
    result[...] = convolved(spread, weight, copies, height + 2, breadth) + table[CONV_BIAS : CONV_BIAS + 1]
    away = pltpu.make_async_copy(result, out, sems.at[3])
    away.start()
    total, squares = column_sums(result[breadth : (1 + height) * breadth, :])
    packed[...] = jnp.broadcast_to(packed_moments(total, squares), packed.shape)
    away.wait()


def first_convolution(height, breadth, below, own, above, sums, table, weight):
    channels = own.shape[1]
    count = sums.shape[0]
    return pl.pallas_call(
        functools.partial(first_kernel, height, breadth),
        in_specs=[NEAR] * 5 + [FAR],
        out_specs=(FAR, NEAR),
        out_shape=(
            jax.ShapeDtypeStruct(((height + 2) * breadth, channels), jnp.float32),
            jax.ShapeDtypeStruct((count, LANES), jnp.float32),
        ),
        scratch_shapes=[
            pltpu.VMEM((3, 3 * channels, channels), jnp.bfloat16),
            pltpu.VMEM(((height + 4) * breadth, 3 * channels), jnp.bfloat16),
            pltpu.VMEM((breadth + 16, channels), jnp.float32),
            pltpu.VMEM(((height + 2) * breadth, channels), jnp.float32),
            pltpu.SemaphoreType.DMA((4,)),
        ],
        compiler_params=pltpu.CompilerParams(vmem_limit_bytes=VMEM_BYTES),
    )(below, own, above, sums, table, weight.reshape(3, 3 * channels, channels))


def second_kernel(
    height, breadth, first, own, sums, table, film, taps, pooled, sent, rows, weight, spread, lines, pairs, sems
):
    count = lax.axis_size("lat")
    place = lax.axis_index("lat")
    channels = own.shape[1]
    spans = [pl.ds(row * breadth, breadth) for row in range(height + 2)]
    copies = fetched(
        [(first.at[span], rows.at[span]) for span in spans]
        + [(taps.at[tap], weight.at[tap]) for tap in range(3)],
        sems,
    )
    lines[...] = jnp.zeros_like(lines)
    center, variance = unpacked_moments(
        sums[...], count * height * breadth * (channels // GROUPS), channels
    )
    factor = lax.rsqrt(variance + eps) * table[GAIN + 1 : GAIN + 2]
    offset = table[BIAS + 1 : BIAS + 2]
    scale = 1.0 + film[:, :channels]
    shift = film[:, channels:]
    for row in range(height + 2):
        copies[row].wait()
        values = rows[row * breadth : (row + 1) * breadth, :]
        values = silu(((values - center) * factor + offset) * scale + shift)
        if row == 0:
            values = jnp.where(place > 0, values, 0.0)
        elif row == height + 1:
            values = jnp.where(place < count - 1, values, 0.0)
        shifted(values, breadth, lines, spread.at[row * breadth : (row + 1) * breadth, :])
    result = convolved(spread, weight, copies[height + 2 :], height, breadth)
    level = ((own[...].astype(jnp.float32) + result + table[CONV_BIAS + 1 : CONV_BIAS + 2]) * skip_gain).astype(jnp.bfloat16)
    level = level.astype(jnp.float32)
    half = breadth // 2
    for row in range(height // 2):
        start = 2 * row * breadth
        both = level[start : start + breadth] + level[start + breadth : start + 2 * breadth]
        for tile in range(channels // LANES):
            lanes = slice(tile * LANES, (tile + 1) * LANES)
            pairs[...] = both[:, lanes]
            mean = (pairs[pl.ds(0, half, stride=2), :] + pairs[pl.ds(1, half, stride=2), :]) * 0.25
            pooled[row * half : (row + 1) * half, lanes] = mean
            sent[row * half : (row + 1) * half, lanes] = mean.astype(jnp.bfloat16)


def second_convolution(height, breadth, first, own, sums, table, film, weight):
    channels = own.shape[1]
    tokens = (height // 2) * (breadth // 2)
    return pl.pallas_call(
        functools.partial(second_kernel, height, breadth),
        in_specs=[FAR] + [NEAR] * 4 + [FAR],
        out_shape=(
            jax.ShapeDtypeStruct((tokens, channels), jnp.float32),
            jax.ShapeDtypeStruct((tokens, channels), jnp.bfloat16),
        ),
        scratch_shapes=[
            pltpu.VMEM(first.shape, jnp.float32),
            pltpu.VMEM((3, 3 * channels, channels), jnp.bfloat16),
            pltpu.VMEM(((height + 2) * breadth, 3 * channels), jnp.bfloat16),
            pltpu.VMEM((breadth + 16, channels), jnp.float32),
            pltpu.VMEM((breadth, LANES), jnp.float32),
            pltpu.SemaphoreType.DMA((height + 5,)),
        ],
        compiler_params=pltpu.CompilerParams(vmem_limit_bytes=VMEM_BYTES),
    )(first, own, sums, table, film, weight.reshape(3, 3 * channels, channels))


def exchange(block, stride):
    count = lax.axis_size("lat")
    return lax.ppermute(block, "lat", [(i, i ^ stride) for i in range(count)])


def gather_blocks(block):
    count = lax.axis_size("lat")
    slow = [block] + [exchange(block, stride) for stride in range(4, count, 4)]
    wide = slow + [exchange(each, 2) for each in slow]
    return wide + [exchange(each, 1) for each in wide]


def attention_kernel(count, *refs):
    blocks = refs[:count]
    pooled, table, qkv_weight, proj_weight, out, keys, values = refs[count:]
    tokens, channels = pooled.shape
    group_width = channels // GROUPS
    sums = jnp.zeros((8, channels), jnp.float32)
    squares = jnp.zeros((8, channels), jnp.float32)
    for block in blocks:
        entry = block[...].astype(jnp.float32).reshape(tokens // 8, 8, channels)
        sums = sums + jnp.sum(entry, axis=0)
        squares = squares + jnp.sum(entry * entry, axis=0)
    sums = jnp.sum(sums, axis=0, keepdims=True)
    squares = jnp.sum(squares, axis=0, keepdims=True)
    row = lax.broadcasted_iota(jnp.int32, (8, channels), 0)
    moments = group_total(jnp.where(row == 0, sums, squares)) / (count * tokens * group_width)
    center = moments[0:1]
    spread = moments[1:2] - center * center
    factor = lax.rsqrt(spread + eps) * table[GAIN + 2 : GAIN + 3]
    offset = table[BIAS + 2 : BIAS + 3]

    def normed(entry):
        return ((entry.astype(jnp.float32) - center) * factor + offset).astype(jnp.bfloat16)

    for i, block in enumerate(blocks):
        projected = jnp.dot(
            normed(block[...]), qkv_weight[:, channels:], preferred_element_type=jnp.float32
        ).astype(jnp.bfloat16)
        keys[i * tokens : (i + 1) * tokens, :] = projected[:, :channels]
        values[i * tokens : (i + 1) * tokens, :] = projected[:, channels:]
    queries = jnp.dot(
        normed(pooled[...]), qkv_weight[:, :channels], preferred_element_type=jnp.float32
    ).astype(jnp.bfloat16) * jnp.bfloat16(HEAD_DIM ** (-0.5))
    first = lax.broadcasted_iota(jnp.int32, (tokens, 2 * HEAD_DIM), 1) < HEAD_DIM
    attended = []
    for start in range(0, channels, 2 * HEAD_DIM):
        pair = slice(start, start + 2 * HEAD_DIM)
        query = queries[:, pair]
        zero = jnp.zeros_like(query)
        both = jnp.concatenate([jnp.where(first, query, zero), jnp.where(first, zero, query)], axis=0)
        scores = lax.dot_general(
            both, keys[:, pair], (((1,), (1,)), ((), ())), preferred_element_type=jnp.float32
        )
        weights = jnp.exp(scores - jnp.max(scores, axis=1, keepdims=True))
        totals = jnp.sum(weights, axis=1, keepdims=True)
        blended = (
            jnp.dot(weights.astype(jnp.bfloat16), values[:, pair], preferred_element_type=jnp.float32)
            / totals
        )
        attended.append(jnp.where(first, blended[:tokens], blended[tokens:]).astype(jnp.bfloat16))
    projected = jnp.dot(
        jnp.concatenate(attended, axis=1), proj_weight[...], preferred_element_type=jnp.float32
    )
    out[...] = ((pooled[...] + projected + table[PROJ_BIAS : PROJ_BIAS + 1]) * skip_gain).astype(jnp.bfloat16)


def attention(blocks, pooled, table, qkv_weight, proj_weight):
    tokens, channels = pooled.shape
    count = len(blocks)
    return pl.pallas_call(
        functools.partial(attention_kernel, count),
        out_shape=jax.ShapeDtypeStruct((tokens, channels), jnp.bfloat16),
        scratch_shapes=[
            pltpu.VMEM((count * tokens, channels), jnp.bfloat16),
            pltpu.VMEM((count * tokens, channels), jnp.bfloat16),
        ],
        compiler_params=pltpu.CompilerParams(vmem_limit_bytes=(12 + count) * 1024 * 1024),
    )(
        *blocks,
        pooled,
        table,
        qkv_weight,
        proj_weight,
    )


def local(
    features,
    noise_index,
    sigma_table,
    affine_weight,
    norm_gain,
    norm_bias,
    conv1_weight,
    conv2_weight,
    conv_bias,
    qkv_weight,
    proj_weight,
    proj_bias,
):
    members, height, breadth, channels = features.shape
    count = lax.axis_size("lat")
    below = lax.ppermute(features[:, -2:], "lat", [(i, i + 1) for i in range(count - 1)])
    above = lax.ppermute(features[:, :2], "lat", [(i + 1, i) for i in range(count - 1)])
    film = noise_terms(noise_index, sigma_table, affine_weight)
    own = features.reshape(height * breadth, channels)
    below = below.reshape(2 * breadth, channels)
    above = above.reshape(2 * breadth, channels)
    table = jnp.concatenate([norm_gain, norm_bias, conv_bias, proj_bias[None]], axis=0)
    packed, own = moments(own)
    first, packed = first_convolution(height, breadth, below, own, above, shared(packed), table, conv1_weight)
    pooled, sent = second_convolution(
        height, breadth, first, own, shared(packed), table, film, conv2_weight
    )
    out = attention(gather_blocks(sent), pooled, table, qkv_weight, proj_weight)
    return out.reshape(members, height // 2, breadth // 2, channels)


def solution(mesh):
    return jax.shard_map(
        local,
        mesh=mesh,
        in_specs=(
            P("grp", "lat", None, None),
            P("grp"),
            P(),
            P(),
            P(),
            P(),
            P(),
            P(),
            P(),
            P(),
            P(),
            P(),
        ),
        out_specs=P("grp", "lat", None, None),
        check_vma=False,
    )
```

```python
import functools
import math

import jax
import jax.numpy as jnp
from jax import lax
from jax.experimental import pallas as pl
from jax.experimental.pallas import tpu as pltpu
from jax.sharding import PartitionSpec as P

HEAD_DIM = 64
GROUPS = 32
FREQS = 64
GROUP_WIDTH = 16
LANES = 128
GAIN, BIAS, CONV_BIAS, PROJ_BIAS = 0, 3, 6, 8
VMEM_BYTES = 52 * 1024 * 1024
SHADOW_BYTES = 256 * 1024 * 1024
FAR = pl.BlockSpec(memory_space=pltpu.HBM)
NEAR = pl.BlockSpec(memory_space=pltpu.VMEM)


eps = 1e-05
skip_gain = 0.7071067811865476


def film_kernel(noise_index, sigma_table, affine_weight, after, out):
    del after
    level = lax.broadcasted_iota(jnp.int32, sigma_table.shape, 1)
    chosen = jnp.where(level == noise_index[0], sigma_table[...], 0.0)
    log_level = jnp.log(jnp.sum(chosen, axis=1, keepdims=True)) / 4.0
    lane = lax.broadcasted_iota(jnp.int32, (1, 2 * FREQS), 1)
    order = (lane % FREQS).astype(jnp.float32)
    angles = log_level * jnp.exp(-math.log(10000.0) * order / FREQS)
    fourier = jnp.where(lane < FREQS, jnp.cos(angles), jnp.sin(angles)).astype(jnp.bfloat16)
    out[...] = jnp.dot(fourier, affine_weight[...], preferred_element_type=jnp.float32)


def film_terms(noise_index, sigma_table, affine_weight, after):
    return pl.pallas_call(
        film_kernel,
        in_specs=[pl.BlockSpec(memory_space=pltpu.SMEM), NEAR, NEAR, FAR],
        out_shape=jax.ShapeDtypeStruct((1, affine_weight.shape[1]), jnp.float32),
        compiler_params=pltpu.CompilerParams(vmem_limit_bytes=VMEM_BYTES),
    )(noise_index, sigma_table[None], affine_weight, after)


def group_total(rows):
    width = rows.shape[1]
    lane = lax.broadcasted_iota(jnp.int32, rows.shape, 1)
    step = 1
    while step < GROUP_WIDTH:
        below = pltpu.roll(rows, step, 1)
        above = pltpu.roll(rows, width - step, 1)
        rows = rows + jnp.where((lane & step) != 0, below, above)
        step *= 2
    return rows


def packed_moments(sums, squares):
    channels = sums.shape[1]
    row = lax.broadcasted_iota(jnp.int32, (8, channels), 0)
    totals = group_total(jnp.where(row == 0, sums, squares))
    slot = lax.broadcasted_iota(jnp.int32, (1, LANES), 1) % GROUP_WIDTH
    packed = jnp.zeros((1, LANES), jnp.float32)
    for tile in range(channels // LANES):
        for kind in range(2):
            part = totals[kind : kind + 1, tile * LANES : (tile + 1) * LANES]
            packed = jnp.where(slot == 2 * tile + kind, part, packed)
    return packed


def unpacked_moments(shared, entries, channels):
    packed = jnp.sum(shared, axis=0, keepdims=True)
    row = lax.broadcasted_iota(jnp.int32, (8, LANES), 0)
    slot = lax.broadcasted_iota(jnp.int32, (8, LANES), 1) % GROUP_WIDTH
    totals = group_total(jnp.where(row == slot, packed, 0.0)) / entries
    tiles = channels // LANES
    center = jnp.concatenate([totals[2 * tile : 2 * tile + 1] for tile in range(tiles)], axis=1)
    second = jnp.concatenate([totals[2 * tile + 1 : 2 * tile + 2] for tile in range(tiles)], axis=1)
    return center, second - center * center


def column_sums(values):
    rows, channels = values.shape
    folded = values.reshape(rows // 8, 8, channels)
    sums = jnp.sum(folded, axis=0)
    squares = jnp.sum(folded * folded, axis=0)
    return jnp.sum(sums, axis=0, keepdims=True), jnp.sum(squares, axis=0, keepdims=True)


def silu(values):
    return values / (1.0 + jnp.exp(-values))


def shared(rows):
    count, lanes = rows.shape
    return lax.all_to_all(rows.reshape(count, 1, lanes), "lat", 0, 0).reshape(count, lanes)


def fetched(pairs, sems):
    copies = [pltpu.make_async_copy(source, target, sems.at[i]) for i, (source, target) in enumerate(pairs)]
    for each in copies:
        each.start()
    return copies


def moments_kernel(parts, features, out, held, sems):
    rows = features.shape[0] // parts
    spans = [pl.ds(part * rows, rows) for part in range(parts)]
    copies = fetched([(features.at[span], held.at[span]) for span in spans], sems)
    sums, squares = 0.0, 0.0
    for part, copy in enumerate(copies):
        copy.wait()
        more = column_sums(held[part * rows : (part + 1) * rows, :].astype(jnp.float32))
        sums, squares = sums + more[0], squares + more[1]
    out[...] = jnp.broadcast_to(packed_moments(sums, squares), out.shape)


def moments(features):
    parts = 4
    return pl.pallas_call(
        functools.partial(moments_kernel, parts),
        in_specs=[FAR],
        out_shape=(
            jax.ShapeDtypeStruct((lax.axis_size("lat"), LANES), jnp.float32),
            jax.ShapeDtypeStruct(features.shape, features.dtype),
        ),
        scratch_shapes=[pltpu.SemaphoreType.DMA((parts,))],
        compiler_params=pltpu.CompilerParams(vmem_limit_bytes=VMEM_BYTES),
    )(features)


def shifted(line, breadth, lines, spread):
    channels = line.shape[1]
    lines[8 : 8 + breadth, :] = line
    spread[:, channels : 2 * channels] = line.astype(jnp.bfloat16)
    spread[:, :channels] = lines[7 : 7 + breadth, :].astype(jnp.bfloat16)
    spread[:, 2 * channels :] = lines[9 : 9 + breadth, :].astype(jnp.bfloat16)


def affine_kernel(which, entries, sums, table, *refs):
    film, out = (None, *refs)[-2:]
    channels = table.shape[1]
    center, variance = unpacked_moments(sums[...], entries, channels)
    factor = lax.rsqrt(variance + eps) * table[GAIN + which : GAIN + which + 1]
    offset = table[BIAS + which : BIAS + which + 1]
    if film is not None:
        scale = 1.0 + film[:, :channels]
        factor = factor * scale
        offset = offset * scale + film[:, channels:]
    out[0:1, :] = center
    out[1:2, :] = factor
    out[2:3, :] = offset


def affine(which, cells, sums, table, *film):
    channels = table.shape[1]
    entries = sums.shape[0] * cells * (channels // GROUPS)
    return pl.pallas_call(
        functools.partial(affine_kernel, which, entries),
        out_shape=jax.ShapeDtypeStruct((3, channels), jnp.float32),
        cost_estimate=pl.CostEstimate(flops=0, bytes_accessed=SHADOW_BYTES, transcendentals=0),
        compiler_params=pltpu.CompilerParams(vmem_limit_bytes=VMEM_BYTES),
    )(sums, table, *film)


def tap_copies(source, target, sems):
    return [pltpu.make_async_copy(source.at[tap], target.at[tap], sems.at[tap]) for tap in range(3)]


def convolved(patches, weight, copies):
    total = None
    for tap, copy in enumerate(copies):
        copy.wait()
        part = jnp.dot(patches(tap), weight[tap], preferred_element_type=jnp.float32)
        total = part if total is None else total + part
    return total


def first_kernel(height, breadth, outer, own, norm, table, taps, mate, other, *refs):
    refs = list(refs)
    if outer:
        refs.pop(0)
    result = refs.pop(0)
    packed = None if outer else refs.pop(0)
    weight, spread, lines, sems = refs
    count = lax.axis_size("lat")
    place = lax.axis_index("lat")
    odd = place % 2 == 1
    channels = own.shape[1]
    copies = tap_copies(taps, weight, sems)
    copies[0].start()
    lines[...] = jnp.zeros_like(lines)
    center, factor, offset = norm[0:1, :], norm[1:2, :], norm[2:3, :]
    if outer:
        needed = [-2, -1, 0, height - 1, height, height + 1]
    else:
        needed = list(range(-1, height + 1))
    for i, row in enumerate(needed):
        if row < 0:
            span = slice((row + height) * breadth, (row + height + 1) * breadth)
            values = jnp.where(odd, mate[span, :], other[span, :])
        elif row < height:
            values = own[row * breadth : (row + 1) * breadth, :]
        else:
            span = slice((row - height) * breadth, (row - height + 1) * breadth)
            values = jnp.where(odd, other[span, :], mate[span, :])
        values = silu((values.astype(jnp.float32) - center) * factor + offset)
        if row < 0:
            values = jnp.where(place > 0, values, 0.0)
        elif row >= height:
            values = jnp.where(place < count - 1, values, 0.0)
        shifted(values, breadth, lines, spread.at[i * breadth : (i + 1) * breadth, :])
        if i in (1, 3):
            copies[(i + 1) // 2].start()

    def patches(tap):
        if outer:
            pair = [spread[(tap + at) * breadth : (tap + at + 1) * breadth, :] for at in (0, 3)]
            return jnp.concatenate(pair, axis=0)
        return spread[tap * breadth : (tap + height) * breadth, :]

    result[...] = convolved(patches, weight, copies) + table[CONV_BIAS : CONV_BIAS + 1]
    if not outer:
        total, squares = column_sums(result[...])
        packed[...] = jnp.broadcast_to(packed_moments(total, squares), packed.shape)


def first_convolution(height, breadth, own, norm, table, weight, mate, other, after=()):
    channels = own.shape[1]
    count = lax.axis_size("lat")
    outer = len(after) > 0
    rows, needed = (2, 6) if outer else (height, height + 2)
    shape = jax.ShapeDtypeStruct((rows * breadth, channels), jnp.float32)
    return pl.pallas_call(
        functools.partial(first_kernel, height, breadth, outer),
        in_specs=[NEAR] * 3 + [FAR] + [NEAR] * 2 + [FAR] * len(after),
        out_shape=shape if outer else (shape, jax.ShapeDtypeStruct((count, LANES), jnp.float32)),
        scratch_shapes=[
            pltpu.VMEM((3, 3 * channels, channels), jnp.bfloat16),
            pltpu.VMEM((needed * breadth, 3 * channels), jnp.bfloat16),
            pltpu.VMEM((breadth + 16, channels), jnp.float32),
            pltpu.SemaphoreType.DMA((3,)),
        ],
        compiler_params=pltpu.CompilerParams(vmem_limit_bytes=VMEM_BYTES),
    )(own, norm, table, weight.reshape(3, 3 * channels, channels), mate, other, *after)


def second_kernel(
    height, breadth, first, outer, own, norm, table, taps, pooled, sent, rows, weight, spread, lines, pairs, sems, weight_sems
):
    count = lax.axis_size("lat")
    place = lax.axis_index("lat")
    channels = own.shape[1]
    low, high = rows.at[pl.ds(0, breadth)], rows.at[pl.ds((height + 1) * breadth, breadth)]
    copies = fetched(
        [
            (first, rows.at[pl.ds(breadth, height * breadth)]),
            (outer.at[pl.ds(0, breadth)], low),
            (outer.at[pl.ds(breadth, breadth)], high),
        ],
        sems,
    )
    weights = tap_copies(taps, weight, weight_sems)
    weights[0].start()
    lines[...] = jnp.zeros_like(lines)
    center, factor, offset = norm[0:1, :], norm[1:2, :], norm[2:3, :]
    for row in [*range(1, height + 1), 0, height + 1]:
        if row in (0, 1, height + 1):
            copies[{1: 0, 0: 1}.get(row, 2)].wait()
        values = rows[row * breadth : (row + 1) * breadth, :]
        values = silu((values - center) * factor + offset)
        if row == 0:
            values = jnp.where(place > 0, values, 0.0)
        elif row == height + 1:
            values = jnp.where(place < count - 1, values, 0.0)
        shifted(values, breadth, lines, spread.at[row * breadth : (row + 1) * breadth, :])
        if row in (2, height + 1):
            weights[1 if row == 2 else 2].start()
    result = convolved(
        lambda tap: spread[tap * breadth : (tap + height) * breadth, :], weight, weights
    )
    level = own[...].astype(jnp.float32) + result + table[CONV_BIAS + 1 : CONV_BIAS + 2]
    level = (level * skip_gain).astype(jnp.bfloat16).astype(jnp.float32)
    half = breadth // 2
    for row in range(height // 2):
        start = 2 * row * breadth
        both = level[start : start + breadth] + level[start + breadth : start + 2 * breadth]
        for tile in range(channels // LANES):
            lanes = slice(tile * LANES, (tile + 1) * LANES)
            pairs[...] = both[:, lanes]
            mean = (pairs[pl.ds(0, half, stride=2), :] + pairs[pl.ds(1, half, stride=2), :]) * 0.25
            pooled[row * half : (row + 1) * half, lanes] = mean
            sent[row * half : (row + 1) * half, lanes] = mean.astype(jnp.bfloat16)


def second_convolution(height, breadth, first, outer, own, norm, table, weight):
    channels = own.shape[1]
    tokens = (height // 2) * (breadth // 2)
    return pl.pallas_call(
        functools.partial(second_kernel, height, breadth),
        in_specs=[FAR] * 2 + [NEAR] * 3 + [FAR],
        out_shape=(
            jax.ShapeDtypeStruct((tokens, channels), jnp.float32),
            jax.ShapeDtypeStruct((tokens, channels), jnp.bfloat16),
        ),
        scratch_shapes=[
            pltpu.VMEM(((height + 2) * breadth, channels), jnp.float32),
            pltpu.VMEM((3, 3 * channels, channels), jnp.bfloat16),
            pltpu.VMEM(((height + 2) * breadth, 3 * channels), jnp.bfloat16),
            pltpu.VMEM((breadth + 16, channels), jnp.float32),
            pltpu.VMEM((breadth, LANES), jnp.float32),
            pltpu.SemaphoreType.DMA((3,)),
            pltpu.SemaphoreType.DMA((3,)),
        ],
        compiler_params=pltpu.CompilerParams(vmem_limit_bytes=VMEM_BYTES),
    )(first, outer, own, norm, table, weight.reshape(3, 3 * channels, channels))


def exchange(block, stride):
    count = lax.axis_size("lat")
    return lax.ppermute(block, "lat", [(i, i ^ stride) for i in range(count)])


def gather_blocks(block):
    count = lax.axis_size("lat")
    slow = [block] + [exchange(block, stride) for stride in range(4, count, 4)]
    wide = slow + [exchange(each, 2) for each in slow]
    return wide + [exchange(each, 1) for each in wide]


def attention_kernel(count, *refs):
    blocks = refs[:count]
    pooled, table, qkv_weight, proj_weight, out, keys, values = refs[count:]
    tokens, channels = pooled.shape
    group_width = channels // GROUPS
    sums = jnp.zeros((8, channels), jnp.float32)
    squares = jnp.zeros((8, channels), jnp.float32)
    for block in blocks:
        entry = block[...].astype(jnp.float32).reshape(tokens // 8, 8, channels)
        sums = sums + jnp.sum(entry, axis=0)
        squares = squares + jnp.sum(entry * entry, axis=0)
    sums = jnp.sum(sums, axis=0, keepdims=True)
    squares = jnp.sum(squares, axis=0, keepdims=True)
    row = lax.broadcasted_iota(jnp.int32, (8, channels), 0)
    moments = group_total(jnp.where(row == 0, sums, squares)) / (count * tokens * group_width)
    center = moments[0:1]
    spread = moments[1:2] - center * center
    factor = lax.rsqrt(spread + eps) * table[GAIN + 2 : GAIN + 3]
    offset = table[BIAS + 2 : BIAS + 3]

    def normed(entry):
        return ((entry.astype(jnp.float32) - center) * factor + offset).astype(jnp.bfloat16)

    for i, block in enumerate(blocks):
        projected = jnp.dot(
            normed(block[...]), qkv_weight[:, channels:], preferred_element_type=jnp.float32
        ).astype(jnp.bfloat16)
        keys[i * tokens : (i + 1) * tokens, :] = projected[:, :channels]
        values[i * tokens : (i + 1) * tokens, :] = projected[:, channels:]
    queries = jnp.dot(
        normed(pooled[...]), qkv_weight[:, :channels], preferred_element_type=jnp.float32
    ).astype(jnp.bfloat16) * jnp.bfloat16(HEAD_DIM ** (-0.5))
    first = lax.broadcasted_iota(jnp.int32, (tokens, 2 * HEAD_DIM), 1) < HEAD_DIM
    attended = []
    for start in range(0, channels, 2 * HEAD_DIM):
        pair = slice(start, start + 2 * HEAD_DIM)
        query = queries[:, pair]
        zero = jnp.zeros_like(query)
        both = jnp.concatenate([jnp.where(first, query, zero), jnp.where(first, zero, query)], axis=0)
        scores = lax.dot_general(
            both, keys[:, pair], (((1,), (1,)), ((), ())), preferred_element_type=jnp.float32
        )
        weights = jnp.exp(scores - jnp.max(scores, axis=1, keepdims=True))
        totals = jnp.sum(weights, axis=1, keepdims=True)
        blended = (
            jnp.dot(weights.astype(jnp.bfloat16), values[:, pair], preferred_element_type=jnp.float32)
            / totals
        )
        attended.append(jnp.where(first, blended[:tokens], blended[tokens:]).astype(jnp.bfloat16))
    projected = jnp.dot(
        jnp.concatenate(attended, axis=1), proj_weight[...], preferred_element_type=jnp.float32
    )
    out[...] = ((pooled[...] + projected + table[PROJ_BIAS : PROJ_BIAS + 1]) * skip_gain).astype(jnp.bfloat16)


def attention(blocks, pooled, table, qkv_weight, proj_weight):
    tokens, channels = pooled.shape
    count = len(blocks)
    return pl.pallas_call(
        functools.partial(attention_kernel, count),
        out_shape=jax.ShapeDtypeStruct((tokens, channels), jnp.bfloat16),
        scratch_shapes=[
            pltpu.VMEM((count * tokens, channels), jnp.bfloat16),
            pltpu.VMEM((count * tokens, channels), jnp.bfloat16),
        ],
        compiler_params=pltpu.CompilerParams(vmem_limit_bytes=(12 + count) * 1024 * 1024),
    )(
        *blocks,
        pooled,
        table,
        qkv_weight,
        proj_weight,
    )


def local(
    features,
    noise_index,
    sigma_table,
    affine_weight,
    norm_gain,
    norm_bias,
    conv1_weight,
    conv2_weight,
    conv_bias,
    qkv_weight,
    proj_weight,
    proj_bias,
):
    members, height, breadth, channels = features.shape
    count = lax.axis_size("lat")
    table = jnp.concatenate([norm_gain, norm_bias, conv_bias, proj_bias[None]], axis=0)
    packed, own = moments(features.reshape(height * breadth, channels))
    mate = lax.ppermute(own, "lat", [(i, i ^ 1) for i in range(count)])
    other = lax.ppermute(own, "lat", [(i, (i - 1 ^ 1) + 1) for i in range(1, count - 1)])
    norm = affine(0, height * breadth, shared(packed), table)
    known = (own, norm, table, conv1_weight, mate, other)
    first, packed = first_convolution(height, breadth, *known)
    outer = first_convolution(height, breadth, *known, [packed])
    film = film_terms(noise_index, sigma_table, affine_weight, packed)
    norm = affine(1, height * breadth, shared(packed), table, film)
    pooled, sent = second_convolution(height, breadth, first, outer, own, norm, table, conv2_weight)
    out = attention(gather_blocks(sent), pooled, table, qkv_weight, proj_weight)
    return out.reshape(members, height // 2, breadth // 2, channels)


def solution(mesh):
    return jax.shard_map(
        local,
        mesh=mesh,
        in_specs=(
            P("grp", "lat", None, None),
            P("grp"),
            P(),
            P(),
            P(),
            P(),
            P(),
            P(),
            P(),
            P(),
            P(),
            P(),
        ),
        out_specs=P("grp", "lat", None, None),
        check_vma=False,
    )
```

```python
import functools
import math

import jax
import jax.numpy as jnp
from jax import lax
from jax.experimental import pallas as pl
from jax.experimental.pallas import tpu as pltpu
from jax.sharding import PartitionSpec as P

HEAD_DIM = 64
GROUPS = 32
FREQS = 64
GROUP_WIDTH = 16
LANES = 128
GAIN, BIAS, CONV_BIAS, PROJ_BIAS = 0, 3, 6, 8
VMEM_BYTES = 52 * 1024 * 1024
SHADOW_BYTES = 256 * 1024 * 1024
FAR = pl.BlockSpec(memory_space=pltpu.HBM)
NEAR = pl.BlockSpec(memory_space=pltpu.VMEM)


eps = 1e-05
skip_gain = 0.7071067811865476


def film_kernel(noise_index, sigma_table, affine_weight, after, out):
    del after
    level = lax.broadcasted_iota(jnp.int32, sigma_table.shape, 1)
    chosen = jnp.where(level == noise_index[0], sigma_table[...], 0.0)
    log_level = jnp.log(jnp.sum(chosen, axis=1, keepdims=True)) / 4.0
    lane = lax.broadcasted_iota(jnp.int32, (1, 2 * FREQS), 1)
    order = (lane % FREQS).astype(jnp.float32)
    angles = log_level * jnp.exp(-math.log(10000.0) * order / FREQS)
    fourier = jnp.where(lane < FREQS, jnp.cos(angles), jnp.sin(angles)).astype(jnp.bfloat16)
    out[...] = jnp.dot(fourier, affine_weight[...], preferred_element_type=jnp.float32)


def film_terms(noise_index, sigma_table, affine_weight, after):
    return pl.pallas_call(
        film_kernel,
        in_specs=[pl.BlockSpec(memory_space=pltpu.SMEM), NEAR, NEAR, FAR],
        out_shape=jax.ShapeDtypeStruct((1, affine_weight.shape[1]), jnp.float32),
        compiler_params=pltpu.CompilerParams(vmem_limit_bytes=VMEM_BYTES),
    )(noise_index, sigma_table[None], affine_weight, after)


def group_total(rows):
    width = rows.shape[1]
    lane = lax.broadcasted_iota(jnp.int32, rows.shape, 1)
    step = 1
    while step < GROUP_WIDTH:
        below = pltpu.roll(rows, step, 1)
        above = pltpu.roll(rows, width - step, 1)
        rows = rows + jnp.where((lane & step) != 0, below, above)
        step *= 2
    return rows


def packed_moments(sums, squares):
    channels = sums.shape[1]
    row = lax.broadcasted_iota(jnp.int32, (8, channels), 0)
    totals = group_total(jnp.where(row == 0, sums, squares))
    slot = lax.broadcasted_iota(jnp.int32, (1, LANES), 1) % GROUP_WIDTH
    packed = jnp.zeros((1, LANES), jnp.float32)
    for tile in range(channels // LANES):
        for kind in range(2):
            part = totals[kind : kind + 1, tile * LANES : (tile + 1) * LANES]
            packed = jnp.where(slot == 2 * tile + kind, part, packed)
    return packed


def unpacked_moments(shared, entries, channels):
    packed = jnp.sum(shared, axis=0, keepdims=True)
    row = lax.broadcasted_iota(jnp.int32, (8, LANES), 0)
    slot = lax.broadcasted_iota(jnp.int32, (8, LANES), 1) % GROUP_WIDTH
    totals = group_total(jnp.where(row == slot, packed, 0.0)) / entries
    tiles = channels // LANES
    center = jnp.concatenate([totals[2 * tile : 2 * tile + 1] for tile in range(tiles)], axis=1)
    second = jnp.concatenate([totals[2 * tile + 1 : 2 * tile + 2] for tile in range(tiles)], axis=1)
    return center, second - center * center


def column_sums(values):
    rows, channels = values.shape
    folded = values.reshape(rows // 8, 8, channels)
    sums = jnp.sum(folded, axis=0)
    squares = jnp.sum(folded * folded, axis=0)
    return jnp.sum(sums, axis=0, keepdims=True), jnp.sum(squares, axis=0, keepdims=True)


def silu(values):
    return values / (1.0 + jnp.exp(-values))


def shared(rows):
    count, lanes = rows.shape
    return lax.all_to_all(rows.reshape(count, 1, lanes), "lat", 0, 0).reshape(count, lanes)


def fetched(pairs, sems):
    copies = [pltpu.make_async_copy(source, target, sems.at[i]) for i, (source, target) in enumerate(pairs)]
    for each in copies:
        each.start()
    return copies


def moments_kernel(features, out, held):
    rows = features.shape[0] // 4
    sums, squares = 0.0, 0.0
    for part in range(4):
        values = features[part * rows : (part + 1) * rows, :]
        held[part * rows : (part + 1) * rows, :] = values
        more = column_sums(values.astype(jnp.float32))
        sums, squares = sums + more[0], squares + more[1]
    out[...] = jnp.broadcast_to(packed_moments(sums, squares), out.shape)


def moments(features):
    return pl.pallas_call(
        moments_kernel,
        out_shape=(
            jax.ShapeDtypeStruct((lax.axis_size("lat"), LANES), jnp.float32),
            jax.ShapeDtypeStruct(features.shape, features.dtype),
        ),
        compiler_params=pltpu.CompilerParams(vmem_limit_bytes=VMEM_BYTES),
    )(features)


def shifted(line, breadth, lines, spread):
    channels = line.shape[1]
    lines[8 : 8 + breadth, :] = line
    spread[:, channels : 2 * channels] = line.astype(jnp.bfloat16)
    spread[:, :channels] = lines[7 : 7 + breadth, :].astype(jnp.bfloat16)
    spread[:, 2 * channels :] = lines[9 : 9 + breadth, :].astype(jnp.bfloat16)


def affine_kernel(which, entries, sums, table, *refs):
    film, out = (None, *refs)[-2:]
    channels = table.shape[1]
    center, variance = unpacked_moments(sums[...], entries, channels)
    factor = lax.rsqrt(variance + eps) * table[GAIN + which : GAIN + which + 1]
    offset = table[BIAS + which : BIAS + which + 1]
    if film is not None:
        scale = 1.0 + film[:, :channels]
        factor = factor * scale
        offset = offset * scale + film[:, channels:]
    out[0:1, :] = center
    out[1:2, :] = factor
    out[2:3, :] = offset


def affine(which, cells, sums, table, *film):
    channels = table.shape[1]
    entries = sums.shape[0] * cells * (channels // GROUPS)
    return pl.pallas_call(
        functools.partial(affine_kernel, which, entries),
        out_shape=jax.ShapeDtypeStruct((3, channels), jnp.float32),
        cost_estimate=pl.CostEstimate(flops=0, bytes_accessed=SHADOW_BYTES, transcendentals=0),
        compiler_params=pltpu.CompilerParams(vmem_limit_bytes=VMEM_BYTES),
    )(sums, table, *film)


def tap_copies(source, target, sems):
    return [pltpu.make_async_copy(source.at[tap], target.at[tap], sems.at[tap]) for tap in range(3)]


def convolved(patches, weight, copies):
    total = None
    for tap, copy in enumerate(copies):
        copy.wait()
        part = jnp.dot(patches(tap), weight[tap], preferred_element_type=jnp.float32)
        total = part if total is None else total + part
    return total


def first_kernel(height, breadth, outer, own, norm, table, taps, mate, other, *refs):
    refs = list(refs)
    if outer:
        refs.pop(0)
    result = refs.pop(0)
    packed = None if outer else refs.pop(0)
    weight, spread, lines, sems = refs
    count = lax.axis_size("lat")
    place = lax.axis_index("lat")
    odd = place % 2 == 1
    channels = own.shape[1]
    copies = tap_copies(taps, weight, sems)
    copies[0].start()
    lines[...] = jnp.zeros_like(lines)
    center, factor, offset = norm[0:1, :], norm[1:2, :], norm[2:3, :]
    if outer:
        needed = [-2, -1, 0, height - 1, height, height + 1]
    else:
        needed = list(range(-1, height + 1))
    for i, row in enumerate(needed):
        if row < 0:
            span = slice((row + height) * breadth, (row + height + 1) * breadth)
            values = jnp.where(odd, mate[span, :], other[span, :])
        elif row < height:
            values = own[row * breadth : (row + 1) * breadth, :]
        else:
            span = slice((row - height) * breadth, (row - height + 1) * breadth)
            values = jnp.where(odd, other[span, :], mate[span, :])
        values = silu((values.astype(jnp.float32) - center) * factor + offset)
        if row < 0:
            values = jnp.where(place > 0, values, 0.0)
        elif row >= height:
            values = jnp.where(place < count - 1, values, 0.0)
        shifted(values, breadth, lines, spread.at[i * breadth : (i + 1) * breadth, :])
        if i in (1, 3):
            copies[(i + 1) // 2].start()

    def patches(tap):
        if outer:
            pair = [spread[(tap + at) * breadth : (tap + at + 1) * breadth, :] for at in (0, 3)]
            return jnp.concatenate(pair, axis=0)
        return spread[tap * breadth : (tap + height) * breadth, :]

    result[...] = convolved(patches, weight, copies) + table[CONV_BIAS : CONV_BIAS + 1]
    if not outer:
        total, squares = column_sums(result[...])
        packed[...] = jnp.broadcast_to(packed_moments(total, squares), packed.shape)


def first_convolution(height, breadth, own, norm, table, weight, mate, other, after=()):
    channels = own.shape[1]
    count = lax.axis_size("lat")
    outer = len(after) > 0
    rows, needed = (2, 6) if outer else (height, height + 2)
    shape = jax.ShapeDtypeStruct((rows * breadth, channels), jnp.float32)
    return pl.pallas_call(
        functools.partial(first_kernel, height, breadth, outer),
        in_specs=[NEAR] * 3 + [FAR] + [NEAR] * 2 + [FAR] * len(after),
        out_shape=shape if outer else (shape, jax.ShapeDtypeStruct((count, LANES), jnp.float32)),
        scratch_shapes=[
            pltpu.VMEM((3, 3 * channels, channels), jnp.bfloat16),
            pltpu.VMEM((needed * breadth, 3 * channels), jnp.bfloat16),
            pltpu.VMEM((breadth + 16, channels), jnp.float32),
            pltpu.SemaphoreType.DMA((3,)),
        ],
        compiler_params=pltpu.CompilerParams(vmem_limit_bytes=VMEM_BYTES),
    )(own, norm, table, weight.reshape(3, 3 * channels, channels), mate, other, *after)


def second_kernel(
    height, breadth, first, outer, own, norm, table, taps, pooled, sent, rows, weight, spread, lines, pairs, sems, weight_sems
):
    count = lax.axis_size("lat")
    place = lax.axis_index("lat")
    channels = own.shape[1]
    low, high = rows.at[pl.ds(0, breadth)], rows.at[pl.ds((height + 1) * breadth, breadth)]
    copies = fetched(
        [
            (first, rows.at[pl.ds(breadth, height * breadth)]),
            (outer.at[pl.ds(0, breadth)], low),
            (outer.at[pl.ds(breadth, breadth)], high),
        ],
        sems,
    )
    weights = tap_copies(taps, weight, weight_sems)
    weights[0].start()
    lines[...] = jnp.zeros_like(lines)
    center, factor, offset = norm[0:1, :], norm[1:2, :], norm[2:3, :]
    for row in [*range(1, height + 1), 0, height + 1]:
        if row in (0, 1, height + 1):
            copies[{1: 0, 0: 1}.get(row, 2)].wait()
        values = rows[row * breadth : (row + 1) * breadth, :]
        values = silu((values - center) * factor + offset)
        if row == 0:
            values = jnp.where(place > 0, values, 0.0)
        elif row == height + 1:
            values = jnp.where(place < count - 1, values, 0.0)
        shifted(values, breadth, lines, spread.at[row * breadth : (row + 1) * breadth, :])
        if row in (2, height + 1):
            weights[1 if row == 2 else 2].start()
    result = convolved(
        lambda tap: spread[tap * breadth : (tap + height) * breadth, :], weight, weights
    )
    level = own[...].astype(jnp.float32) + result + table[CONV_BIAS + 1 : CONV_BIAS + 2]
    level = (level * skip_gain).astype(jnp.bfloat16).astype(jnp.float32)
    half = breadth // 2
    for row in range(height // 2):
        start = 2 * row * breadth
        both = level[start : start + breadth] + level[start + breadth : start + 2 * breadth]
        for tile in range(channels // LANES):
            lanes = slice(tile * LANES, (tile + 1) * LANES)
            pairs[...] = both[:, lanes]
            mean = (pairs[pl.ds(0, half, stride=2), :] + pairs[pl.ds(1, half, stride=2), :]) * 0.25
            pooled[row * half : (row + 1) * half, lanes] = mean
            sent[row * half : (row + 1) * half, lanes] = mean.astype(jnp.bfloat16)


def second_convolution(height, breadth, first, outer, own, norm, table, weight):
    channels = own.shape[1]
    tokens = (height // 2) * (breadth // 2)
    return pl.pallas_call(
        functools.partial(second_kernel, height, breadth),
        in_specs=[FAR] * 2 + [NEAR] * 3 + [FAR],
        out_shape=(
            jax.ShapeDtypeStruct((tokens, channels), jnp.float32),
            jax.ShapeDtypeStruct((tokens, channels), jnp.bfloat16),
        ),
        scratch_shapes=[
            pltpu.VMEM(((height + 2) * breadth, channels), jnp.float32),
            pltpu.VMEM((3, 3 * channels, channels), jnp.bfloat16),
            pltpu.VMEM(((height + 2) * breadth, 3 * channels), jnp.bfloat16),
            pltpu.VMEM((breadth + 16, channels), jnp.float32),
            pltpu.VMEM((breadth, LANES), jnp.float32),
            pltpu.SemaphoreType.DMA((3,)),
            pltpu.SemaphoreType.DMA((3,)),
        ],
        compiler_params=pltpu.CompilerParams(vmem_limit_bytes=VMEM_BYTES),
    )(first, outer, own, norm, table, weight.reshape(3, 3 * channels, channels))


def exchange(block, stride):
    count = lax.axis_size("lat")
    return lax.ppermute(block, "lat", [(i, i ^ stride) for i in range(count)])


def gather_blocks(block):
    count = lax.axis_size("lat")
    slow = [block] + [exchange(block, stride) for stride in range(4, count, 4)]
    wide = slow + [exchange(each, 2) for each in slow]
    return wide + [exchange(each, 1) for each in wide]


def attention_kernel(count, *refs):
    blocks = refs[:count]
    pooled, table, qkv_weight, proj_weight, out, normed, projected = refs[count:]
    tokens, channels = pooled.shape
    sums, squares = 0.0, 0.0
    for block in blocks:
        more = column_sums(block[...].astype(jnp.float32))
        sums, squares = sums + more[0], squares + more[1]
    row = lax.broadcasted_iota(jnp.int32, (8, channels), 0)
    entries = count * tokens * (channels // GROUPS)
    moments = group_total(jnp.where(row == 0, sums, squares)) / entries
    center = moments[0:1]
    factor = lax.rsqrt(moments[1:2] - center * center + eps) * table[GAIN + 2 : GAIN + 3]
    offset = table[BIAS + 2 : BIAS + 3]

    def norm(values):
        return ((values.astype(jnp.float32) - center) * factor + offset).astype(jnp.bfloat16)

    for i, block in enumerate(blocks):
        normed[i * tokens : (i + 1) * tokens, :] = norm(block[...])
    projected[...] = jnp.dot(
        normed[...], qkv_weight[:, channels:], preferred_element_type=jnp.float32
    ).astype(jnp.bfloat16)
    queries = jnp.dot(
        norm(pooled[...]), qkv_weight[:, :channels], preferred_element_type=jnp.float32
    ).astype(jnp.bfloat16) * jnp.bfloat16(HEAD_DIM ** (-0.5))
    first = lax.broadcasted_iota(jnp.int32, (tokens, 2 * HEAD_DIM), 1) < HEAD_DIM
    starts = range(0, channels, 2 * HEAD_DIM)

    def scored(start):
        query = queries[:, start : start + 2 * HEAD_DIM]
        zero = jnp.zeros_like(query)
        both = jnp.concatenate([jnp.where(first, query, zero), jnp.where(first, zero, query)], axis=0)
        keys = projected[:, start : start + 2 * HEAD_DIM]
        return lax.dot_general(both, keys, (((1,), (1,)), ((), ())), preferred_element_type=jnp.float32)

    attended = []
    later = scored(0)
    for start in starts:
        scores = later
        if start + 2 * HEAD_DIM < channels:
            later = scored(start + 2 * HEAD_DIM)
        weights = jnp.exp(scores - jnp.max(scores, axis=1, keepdims=True))
        totals = jnp.sum(weights, axis=1, keepdims=True)
        values = projected[:, channels + start : channels + start + 2 * HEAD_DIM]
        blended = jnp.dot(weights.astype(jnp.bfloat16), values, preferred_element_type=jnp.float32) / totals
        attended.append(jnp.where(first, blended[:tokens], blended[tokens:]).astype(jnp.bfloat16))
    result = jnp.dot(jnp.concatenate(attended, axis=1), proj_weight[...], preferred_element_type=jnp.float32)
    result = pooled[...] + result + table[PROJ_BIAS : PROJ_BIAS + 1]
    out[...] = (result * skip_gain).astype(jnp.bfloat16)


def attention(blocks, pooled, table, qkv_weight, proj_weight):
    tokens, channels = pooled.shape
    count = len(blocks)
    return pl.pallas_call(
        functools.partial(attention_kernel, count),
        out_shape=jax.ShapeDtypeStruct((tokens, channels), jnp.bfloat16),
        scratch_shapes=[
            pltpu.VMEM((count * tokens, channels), jnp.bfloat16),
            pltpu.VMEM((count * tokens, 2 * channels), jnp.bfloat16),
        ],
        compiler_params=pltpu.CompilerParams(vmem_limit_bytes=(12 + count) * 1024 * 1024),
    )(*blocks, pooled, table, qkv_weight, proj_weight)


def local(
    features,
    noise_index,
    sigma_table,
    affine_weight,
    norm_gain,
    norm_bias,
    conv1_weight,
    conv2_weight,
    conv_bias,
    qkv_weight,
    proj_weight,
    proj_bias,
):
    members, height, breadth, channels = features.shape
    count = lax.axis_size("lat")
    table = jnp.concatenate([norm_gain, norm_bias, conv_bias, proj_bias[None]], axis=0)
    packed, own = moments(features.reshape(height * breadth, channels))
    mate = lax.ppermute(own, "lat", [(i, i ^ 1) for i in range(count)])
    other = lax.ppermute(own, "lat", [(i, (i - 1 ^ 1) + 1) for i in range(1, count - 1)])
    norm = affine(0, height * breadth, shared(packed), table)
    known = (own, norm, table, conv1_weight, mate, other)
    first, packed = first_convolution(height, breadth, *known)
    outer = first_convolution(height, breadth, *known, [packed])
    film = film_terms(noise_index, sigma_table, affine_weight, packed)
    norm = affine(1, height * breadth, shared(packed), table, film)
    pooled, sent = second_convolution(height, breadth, first, outer, own, norm, table, conv2_weight)
    out = attention(gather_blocks(sent), pooled, table, qkv_weight, proj_weight)
    return out.reshape(members, height // 2, breadth // 2, channels)


def solution(mesh):
    return jax.shard_map(
        local,
        mesh=mesh,
        in_specs=(
            P("grp", "lat", None, None),
            P("grp"),
            P(),
            P(),
            P(),
            P(),
            P(),
            P(),
            P(),
            P(),
            P(),
            P(),
        ),
        out_specs=P("grp", "lat", None, None),
        check_vma=False,
    )
```

```python
import functools
import math

import jax
import jax.numpy as jnp
from jax import lax
from jax.experimental import pallas as pl
from jax.experimental.pallas import tpu as pltpu
from jax.sharding import PartitionSpec as P

HEAD_DIM = 64
GROUPS = 32
FREQS = 64
GROUP_WIDTH = 16
LANES = 128
GAIN, BIAS, CONV_BIAS, PROJ_BIAS = 0, 3, 6, 8
VMEM_BYTES = 52 * 1024 * 1024
SHADOW_BYTES = 256 * 1024 * 1024
OUTER_BYTES = 52 * 1024 * 1024
SECOND_BYTES = 51 * 1024 * 1024
FAR = pl.BlockSpec(memory_space=pltpu.HBM)
NEAR = pl.BlockSpec(memory_space=pltpu.VMEM)


eps = 1e-05
skip_gain = 0.7071067811865476


def film_kernel(noise_index, sigma_table, affine_weight, after, out):
    del after
    level = lax.broadcasted_iota(jnp.int32, sigma_table.shape, 1)
    chosen = jnp.where(level == noise_index[0], sigma_table[...], 0.0)
    log_level = jnp.log(jnp.sum(chosen, axis=1, keepdims=True)) / 4.0
    lane = lax.broadcasted_iota(jnp.int32, (1, 2 * FREQS), 1)
    order = (lane % FREQS).astype(jnp.float32)
    angles = log_level * jnp.exp(-math.log(10000.0) * order / FREQS)
    fourier = jnp.where(lane < FREQS, jnp.cos(angles), jnp.sin(angles)).astype(jnp.bfloat16)
    out[...] = jnp.dot(fourier, affine_weight[...], preferred_element_type=jnp.float32)


def film_terms(noise_index, sigma_table, affine_weight, after):
    return pl.pallas_call(
        film_kernel,
        in_specs=[pl.BlockSpec(memory_space=pltpu.SMEM), NEAR, NEAR, FAR],
        out_shape=jax.ShapeDtypeStruct((1, affine_weight.shape[1]), jnp.float32),
        compiler_params=pltpu.CompilerParams(vmem_limit_bytes=VMEM_BYTES),
    )(noise_index, sigma_table[None], affine_weight, after)


def group_total(rows):
    width = rows.shape[1]
    lane = lax.broadcasted_iota(jnp.int32, rows.shape, 1)
    step = 1
    while step < GROUP_WIDTH:
        below = pltpu.roll(rows, step, 1)
        above = pltpu.roll(rows, width - step, 1)
        rows = rows + jnp.where((lane & step) != 0, below, above)
        step *= 2
    return rows


def packed_moments(sums, squares):
    channels = sums.shape[1]
    row = lax.broadcasted_iota(jnp.int32, (8, channels), 0)
    totals = group_total(jnp.where(row == 0, sums, squares))
    slot = lax.broadcasted_iota(jnp.int32, (1, LANES), 1) % GROUP_WIDTH
    packed = jnp.zeros((1, LANES), jnp.float32)
    for tile in range(channels // LANES):
        for kind in range(2):
            part = totals[kind : kind + 1, tile * LANES : (tile + 1) * LANES]
            packed = jnp.where(slot == 2 * tile + kind, part, packed)
    return packed


def unpacked_moments(shared, entries, channels):
    packed = jnp.sum(shared, axis=0, keepdims=True)
    row = lax.broadcasted_iota(jnp.int32, (8, LANES), 0)
    slot = lax.broadcasted_iota(jnp.int32, (8, LANES), 1) % GROUP_WIDTH
    totals = group_total(jnp.where(row == slot, packed, 0.0)) / entries
    tiles = channels // LANES
    center = jnp.concatenate([totals[2 * tile : 2 * tile + 1] for tile in range(tiles)], axis=1)
    second = jnp.concatenate([totals[2 * tile + 1 : 2 * tile + 2] for tile in range(tiles)], axis=1)
    return center, second - center * center


def column_sums(values):
    rows, channels = values.shape
    folded = values.reshape(rows // 8, 8, channels)
    sums = jnp.sum(folded, axis=0)
    squares = jnp.sum(folded * folded, axis=0)
    return jnp.sum(sums, axis=0, keepdims=True), jnp.sum(squares, axis=0, keepdims=True)


def silu(values):
    return values / (1.0 + jnp.exp(-values))


def shared(rows):
    count, lanes = rows.shape
    return lax.all_to_all(rows.reshape(count, 1, lanes), "lat", 0, 0).reshape(count, lanes)


def fetched(pairs, sems):
    copies = [pltpu.make_async_copy(source, target, sems.at[i]) for i, (source, target) in enumerate(pairs)]
    for each in copies:
        each.start()
    return copies


def moments_kernel(features, out, held):
    rows = features.shape[0] // 4
    sums, squares = 0.0, 0.0
    for part in range(4):
        values = features[part * rows : (part + 1) * rows, :]
        held[part * rows : (part + 1) * rows, :] = values
        more = column_sums(values.astype(jnp.float32))
        sums, squares = sums + more[0], squares + more[1]
    out[...] = jnp.broadcast_to(packed_moments(sums, squares), out.shape)


def moments(features):
    return pl.pallas_call(
        moments_kernel,
        out_shape=(
            jax.ShapeDtypeStruct((lax.axis_size("lat"), LANES), jnp.float32),
            jax.ShapeDtypeStruct(features.shape, features.dtype),
        ),
        compiler_params=pltpu.CompilerParams(vmem_limit_bytes=VMEM_BYTES),
    )(features)


def shifted(line, spread):
    breadth, channels = line.shape
    column = lax.broadcasted_iota(jnp.int32, line.shape, 0)
    before = jnp.where(column == 0, 0.0, pltpu.roll(line, 1, 0))
    after = jnp.where(column == breadth - 1, 0.0, pltpu.roll(line, breadth - 1, 0))
    spread[:, :channels] = before.astype(jnp.bfloat16)
    spread[:, channels : 2 * channels] = line.astype(jnp.bfloat16)
    spread[:, 2 * channels :] = after.astype(jnp.bfloat16)


def affine_kernel(which, entries, sums, table, *refs):
    film, out = (None, *refs)[-2:]
    channels = table.shape[1]
    center, variance = unpacked_moments(sums[...], entries, channels)
    factor = lax.rsqrt(variance + eps) * table[GAIN + which : GAIN + which + 1]
    offset = table[BIAS + which : BIAS + which + 1]
    if film is not None:
        scale = 1.0 + film[:, :channels]
        factor = factor * scale
        offset = offset * scale + film[:, channels:]
    out[0:1, :] = center
    out[1:2, :] = factor
    out[2:3, :] = offset


def affine(which, cells, sums, table, *film):
    channels = table.shape[1]
    entries = sums.shape[0] * cells * (channels // GROUPS)
    return pl.pallas_call(
        functools.partial(affine_kernel, which, entries),
        out_shape=jax.ShapeDtypeStruct((3, channels), jnp.float32),
        cost_estimate=pl.CostEstimate(flops=0, bytes_accessed=SHADOW_BYTES, transcendentals=0),
        compiler_params=pltpu.CompilerParams(vmem_limit_bytes=VMEM_BYTES),
    )(sums, table, *film)


def tap_copies(source, target, sems):
    return [pltpu.make_async_copy(source.at[tap], target.at[tap], sems.at[tap]) for tap in range(3)]


def convolved(patches, weight, copies):
    total = None
    for tap, copy in enumerate(copies):
        copy.wait()
        part = jnp.dot(patches(tap), weight[tap], preferred_element_type=jnp.float32)
        total = part if total is None else total + part
    return total


def first_kernel(height, breadth, outer, own, norm, table, taps, mate, other, *refs):
    refs = list(refs)
    if outer:
        refs.pop(0)
    result = refs.pop(0)
    packed = None if outer else refs.pop(0)
    weight, spread, sems = refs
    count = lax.axis_size("lat")
    place = lax.axis_index("lat")
    odd = place % 2 == 1
    channels = own.shape[1]
    copies = tap_copies(taps, weight, sems)
    copies[0].start()
    center, factor, offset = norm[0:1, :], norm[1:2, :], norm[2:3, :]
    if outer:
        needed = [-2, -1, 0, height - 1, height, height + 1]
    else:
        needed = list(range(-1, height + 1))
    for i, row in enumerate(needed):
        if row < 0:
            span = slice((row + height) * breadth, (row + height + 1) * breadth)
            values = jnp.where(odd, mate[span, :], other[span, :])
        elif row < height:
            values = own[row * breadth : (row + 1) * breadth, :]
        else:
            span = slice((row - height) * breadth, (row - height + 1) * breadth)
            values = jnp.where(odd, other[span, :], mate[span, :])
        values = silu((values.astype(jnp.float32) - center) * factor + offset)
        if row < 0:
            values = jnp.where(place > 0, values, 0.0)
        elif row >= height:
            values = jnp.where(place < count - 1, values, 0.0)
        shifted(values, spread.at[i * breadth : (i + 1) * breadth, :])
        if i in (1, 3):
            copies[(i + 1) // 2].start()

    def patches(tap):
        if outer:
            pair = [spread[(tap + at) * breadth : (tap + at + 1) * breadth, :] for at in (0, 3)]
            return jnp.concatenate(pair, axis=0)
        return spread[tap * breadth : (tap + height) * breadth, :]

    result[...] = convolved(patches, weight, copies) + table[CONV_BIAS : CONV_BIAS + 1]
    if not outer:
        total, squares = column_sums(result[...])
        packed[...] = jnp.broadcast_to(packed_moments(total, squares), packed.shape)


def first_convolution(height, breadth, own, norm, table, weight, mate, other, after=()):
    channels = own.shape[1]
    count = lax.axis_size("lat")
    outer = len(after) > 0
    rows, needed = (2, 6) if outer else (height, height + 2)
    shape = jax.ShapeDtypeStruct((rows * breadth, channels), jnp.float32)
    return pl.pallas_call(
        functools.partial(first_kernel, height, breadth, outer),
        in_specs=[NEAR] * 3 + [FAR] + [NEAR] * 2 + [FAR] * len(after),
        out_shape=shape if outer else (shape, jax.ShapeDtypeStruct((count, LANES), jnp.float32)),
        scratch_shapes=[
            pltpu.VMEM((3, 3 * channels, channels), jnp.bfloat16),
            pltpu.VMEM((needed * breadth, 3 * channels), jnp.bfloat16),
            pltpu.SemaphoreType.DMA((3,)),
        ],
        compiler_params=pltpu.CompilerParams(vmem_limit_bytes=OUTER_BYTES if outer else VMEM_BYTES),
    )(own, norm, table, weight.reshape(3, 3 * channels, channels), mate, other, *after)


def second_kernel(
    height, breadth, first, outer, own, norm, table, taps, pooled, sent, weight, spread, pairs, sems
):
    count = lax.axis_size("lat")
    place = lax.axis_index("lat")
    channels = own.shape[1]
    weights = tap_copies(taps, weight, sems)
    weights[0].start()
    center, factor, offset = norm[0:1, :], norm[1:2, :], norm[2:3, :]
    for row in [*range(1, height + 1), 0, height + 1]:
        if 0 < row <= height:
            values = first[(row - 1) * breadth : row * breadth, :]
        else:
            at = 0 if row == 0 else breadth
            values = outer[at : at + breadth, :]
        values = silu((values - center) * factor + offset)
        if row == 0:
            values = jnp.where(place > 0, values, 0.0)
        elif row == height + 1:
            values = jnp.where(place < count - 1, values, 0.0)
        shifted(values, spread.at[row * breadth : (row + 1) * breadth, :])
        if row in (2, height + 1):
            weights[1 if row == 2 else 2].start()
    result = convolved(
        lambda tap: spread[tap * breadth : (tap + height) * breadth, :], weight, weights
    )
    level = own[...].astype(jnp.float32) + result + table[CONV_BIAS + 1 : CONV_BIAS + 2]
    level = (level * skip_gain).astype(jnp.bfloat16).astype(jnp.float32)
    half = breadth // 2
    for row in range(height // 2):
        start = 2 * row * breadth
        both = level[start : start + breadth] + level[start + breadth : start + 2 * breadth]
        for tile in range(channels // LANES):
            lanes = slice(tile * LANES, (tile + 1) * LANES)
            pairs[...] = both[:, lanes]
            mean = (pairs[pl.ds(0, half, stride=2), :] + pairs[pl.ds(1, half, stride=2), :]) * 0.25
            pooled[row * half : (row + 1) * half, lanes] = mean
            sent[row * half : (row + 1) * half, lanes] = mean.astype(jnp.bfloat16)


def second_convolution(height, breadth, first, outer, own, norm, table, weight):
    channels = own.shape[1]
    tokens = (height // 2) * (breadth // 2)
    return pl.pallas_call(
        functools.partial(second_kernel, height, breadth),
        in_specs=[NEAR] * 5 + [FAR],
        out_shape=(
            jax.ShapeDtypeStruct((tokens, channels), jnp.float32),
            jax.ShapeDtypeStruct((tokens, channels), jnp.bfloat16),
        ),
        scratch_shapes=[
            pltpu.VMEM((3, 3 * channels, channels), jnp.bfloat16),
            pltpu.VMEM(((height + 2) * breadth, 3 * channels), jnp.bfloat16),
            pltpu.VMEM((breadth, LANES), jnp.float32),
            pltpu.SemaphoreType.DMA((3,)),
        ],
        compiler_params=pltpu.CompilerParams(vmem_limit_bytes=SECOND_BYTES),
    )(first, outer, own, norm, table, weight.reshape(3, 3 * channels, channels))


def exchange(block, stride):
    count = lax.axis_size("lat")
    return lax.ppermute(block, "lat", [(i, i ^ stride) for i in range(count)])


def gather_blocks(block):
    count = lax.axis_size("lat")
    slow = [block] + [exchange(block, stride) for stride in range(4, count, 4)]
    wide = slow + [exchange(each, 2) for each in slow]
    return wide + [exchange(each, 1) for each in wide]


def attention_kernel(count, *refs):
    blocks = refs[:count]
    pooled, table, qkv_weight, proj_weight, out, normed, projected = refs[count:]
    tokens, channels = pooled.shape
    sums, squares = 0.0, 0.0
    for block in blocks:
        more = column_sums(block[...].astype(jnp.float32))
        sums, squares = sums + more[0], squares + more[1]
    row = lax.broadcasted_iota(jnp.int32, (8, channels), 0)
    entries = count * tokens * (channels // GROUPS)
    moments = group_total(jnp.where(row == 0, sums, squares)) / entries
    center = moments[0:1]
    factor = lax.rsqrt(moments[1:2] - center * center + eps) * table[GAIN + 2 : GAIN + 3]
    offset = table[BIAS + 2 : BIAS + 3]

    def norm(values):
        return ((values.astype(jnp.float32) - center) * factor + offset).astype(jnp.bfloat16)

    for i, block in enumerate(blocks):
        normed[i * tokens : (i + 1) * tokens, :] = norm(block[...])
    projected[...] = jnp.dot(
        normed[...], qkv_weight[:, channels:], preferred_element_type=jnp.float32
    ).astype(jnp.bfloat16)
    queries = jnp.dot(
        norm(pooled[...]), qkv_weight[:, :channels], preferred_element_type=jnp.float32
    ).astype(jnp.bfloat16) * jnp.bfloat16(HEAD_DIM ** (-0.5))
    first = lax.broadcasted_iota(jnp.int32, (tokens, 2 * HEAD_DIM), 1) < HEAD_DIM
    starts = range(0, channels, 2 * HEAD_DIM)

    def scored(start):
        query = queries[:, start : start + 2 * HEAD_DIM]
        zero = jnp.zeros_like(query)
        both = jnp.concatenate([jnp.where(first, query, zero), jnp.where(first, zero, query)], axis=0)
        keys = projected[:, start : start + 2 * HEAD_DIM]
        return lax.dot_general(both, keys, (((1,), (1,)), ((), ())), preferred_element_type=jnp.float32)

    attended = []
    later = scored(0)
    for start in starts:
        scores = later
        if start + 2 * HEAD_DIM < channels:
            later = scored(start + 2 * HEAD_DIM)
        weights = jnp.exp(scores - jnp.max(scores, axis=1, keepdims=True))
        totals = jnp.sum(weights, axis=1, keepdims=True)
        values = projected[:, channels + start : channels + start + 2 * HEAD_DIM]
        blended = jnp.dot(weights.astype(jnp.bfloat16), values, preferred_element_type=jnp.float32) / totals
        attended.append(jnp.where(first, blended[:tokens], blended[tokens:]).astype(jnp.bfloat16))
    result = jnp.dot(jnp.concatenate(attended, axis=1), proj_weight[...], preferred_element_type=jnp.float32)
    result = pooled[...] + result + table[PROJ_BIAS : PROJ_BIAS + 1]
    out[...] = (result * skip_gain).astype(jnp.bfloat16)


def attention(blocks, pooled, table, qkv_weight, proj_weight):
    tokens, channels = pooled.shape
    count = len(blocks)
    return pl.pallas_call(
        functools.partial(attention_kernel, count),
        out_shape=jax.ShapeDtypeStruct((tokens, channels), jnp.bfloat16),
        scratch_shapes=[
            pltpu.VMEM((count * tokens, channels), jnp.bfloat16),
            pltpu.VMEM((count * tokens, 2 * channels), jnp.bfloat16),
        ],
        compiler_params=pltpu.CompilerParams(vmem_limit_bytes=(12 + count) * 1024 * 1024),
    )(*blocks, pooled, table, qkv_weight, proj_weight)


def local(
    features,
    noise_index,
    sigma_table,
    affine_weight,
    norm_gain,
    norm_bias,
    conv1_weight,
    conv2_weight,
    conv_bias,
    qkv_weight,
    proj_weight,
    proj_bias,
):
    members, height, breadth, channels = features.shape
    count = lax.axis_size("lat")
    table = jnp.concatenate([norm_gain, norm_bias, conv_bias, proj_bias[None]], axis=0)
    packed, own = moments(features.reshape(height * breadth, channels))
    mate = lax.ppermute(own, "lat", [(i, i ^ 1) for i in range(count)])
    other = lax.ppermute(own, "lat", [(i, (i - 1 ^ 1) + 1) for i in range(1, count - 1)])
    norm = affine(0, height * breadth, shared(packed), table)
    known = (own, norm, table, conv1_weight, mate, other)
    first, packed = first_convolution(height, breadth, *known)
    outer = first_convolution(height, breadth, *known, [packed])
    film = film_terms(noise_index, sigma_table, affine_weight, packed)
    norm = affine(1, height * breadth, shared(packed), table, film)
    pooled, sent = second_convolution(
        height, breadth, first, outer, features.reshape(height * breadth, channels), norm, table, conv2_weight
    )
    out = attention(gather_blocks(sent), pooled, table, qkv_weight, proj_weight)
    return out.reshape(members, height // 2, breadth // 2, channels)


def solution(mesh):
    return jax.shard_map(
        local,
        mesh=mesh,
        in_specs=(
            P("grp", "lat", None, None),
            P("grp"),
            P(),
            P(),
            P(),
            P(),
            P(),
            P(),
            P(),
            P(),
            P(),
            P(),
        ),
        out_specs=P("grp", "lat", None, None),
        check_vma=False,
    )
```

```python
import functools
import math

import jax
import jax.numpy as jnp
from jax import lax
from jax.experimental import pallas as pl
from jax.experimental.pallas import tpu as pltpu
from jax.sharding import PartitionSpec as P

HEAD_DIM = 64
GROUPS = 32
FREQS = 64
GROUP_WIDTH = 16
LANES = 128
GAIN, BIAS, CONV_BIAS, PROJ_BIAS = 0, 3, 6, 8
VMEM_BYTES = 52 * 1024 * 1024
SHADOW_BYTES = 256 * 1024 * 1024
OUTER_BYTES = 52 * 1024 * 1024
SECOND_BYTES = 51 * 1024 * 1024
FAR = pl.BlockSpec(memory_space=pltpu.HBM)
NEAR = pl.BlockSpec(memory_space=pltpu.VMEM)


eps = 1e-05
skip_gain = 0.7071067811865476


def film_kernel(noise_index, sigma_table, affine_weight, after, out):
    del after
    level = lax.broadcasted_iota(jnp.int32, sigma_table.shape, 1)
    chosen = jnp.where(level == noise_index[0], sigma_table[...], 0.0)
    log_level = jnp.log(jnp.sum(chosen, axis=1, keepdims=True)) / 4.0
    lane = lax.broadcasted_iota(jnp.int32, (1, 2 * FREQS), 1)
    order = (lane % FREQS).astype(jnp.float32)
    angles = log_level * jnp.exp(-math.log(10000.0) * order / FREQS)
    fourier = jnp.where(lane < FREQS, jnp.cos(angles), jnp.sin(angles)).astype(jnp.bfloat16)
    out[...] = jnp.dot(fourier, affine_weight[...], preferred_element_type=jnp.float32)


def film_terms(noise_index, sigma_table, affine_weight, after):
    return pl.pallas_call(
        film_kernel,
        in_specs=[pl.BlockSpec(memory_space=pltpu.SMEM), NEAR, NEAR, FAR],
        out_shape=jax.ShapeDtypeStruct((1, affine_weight.shape[1]), jnp.float32),
        compiler_params=pltpu.CompilerParams(vmem_limit_bytes=VMEM_BYTES),
    )(noise_index, sigma_table[None], affine_weight, after)


def group_total(rows):
    width = rows.shape[1]
    lane = lax.broadcasted_iota(jnp.int32, rows.shape, 1)
    step = 1
    while step < GROUP_WIDTH:
        below = pltpu.roll(rows, step, 1)
        above = pltpu.roll(rows, width - step, 1)
        rows = rows + jnp.where((lane & step) != 0, below, above)
        step *= 2
    return rows


def packed_moments(sums, squares):
    channels = sums.shape[1]
    row = lax.broadcasted_iota(jnp.int32, (8, channels), 0)
    totals = group_total(jnp.where(row == 0, sums, squares))
    slot = lax.broadcasted_iota(jnp.int32, (1, LANES), 1) % GROUP_WIDTH
    packed = jnp.zeros((1, LANES), jnp.float32)
    for tile in range(channels // LANES):
        for kind in range(2):
            part = totals[kind : kind + 1, tile * LANES : (tile + 1) * LANES]
            packed = jnp.where(slot == 2 * tile + kind, part, packed)
    return packed


def unpacked_moments(shared, entries, channels):
    packed = jnp.sum(shared, axis=0, keepdims=True)
    row = lax.broadcasted_iota(jnp.int32, (8, LANES), 0)
    slot = lax.broadcasted_iota(jnp.int32, (8, LANES), 1) % GROUP_WIDTH
    totals = group_total(jnp.where(row == slot, packed, 0.0)) / entries
    tiles = channels // LANES
    center = jnp.concatenate([totals[2 * tile : 2 * tile + 1] for tile in range(tiles)], axis=1)
    second = jnp.concatenate([totals[2 * tile + 1 : 2 * tile + 2] for tile in range(tiles)], axis=1)
    return center, second - center * center


def column_sums(values):
    rows, channels = values.shape
    folded = values.reshape(rows // 8, 8, channels)
    sums = jnp.sum(folded, axis=0)
    squares = jnp.sum(folded * folded, axis=0)
    return jnp.sum(sums, axis=0, keepdims=True), jnp.sum(squares, axis=0, keepdims=True)


def silu(values):
    return values / (1.0 + jnp.exp(-values))


def shared(rows):
    count, lanes = rows.shape
    return lax.all_to_all(rows.reshape(count, 1, lanes), "lat", 0, 0).reshape(count, lanes)


def fetched(pairs, sems):
    copies = [pltpu.make_async_copy(source, target, sems.at[i]) for i, (source, target) in enumerate(pairs)]
    for each in copies:
        each.start()
    return copies


def moments_kernel(features, out, held):
    rows = features.shape[0] // 4
    sums, squares = 0.0, 0.0
    for part in range(4):
        values = features[part * rows : (part + 1) * rows, :]
        held[part * rows : (part + 1) * rows, :] = values
        more = column_sums(values.astype(jnp.float32))
        sums, squares = sums + more[0], squares + more[1]
    out[...] = jnp.broadcast_to(packed_moments(sums, squares), out.shape)


def moments(features):
    return pl.pallas_call(
        moments_kernel,
        out_shape=(
            jax.ShapeDtypeStruct((lax.axis_size("lat"), LANES), jnp.float32),
            jax.ShapeDtypeStruct(features.shape, features.dtype),
        ),
        compiler_params=pltpu.CompilerParams(vmem_limit_bytes=VMEM_BYTES),
    )(features)


def shifted(line, spread):
    breadth, channels = line.shape
    column = lax.broadcasted_iota(jnp.int32, line.shape, 0)
    before = jnp.where(column == 0, 0.0, pltpu.roll(line, 1, 0))
    after = jnp.where(column == breadth - 1, 0.0, pltpu.roll(line, breadth - 1, 0))
    spread[:, :channels] = before.astype(jnp.bfloat16)
    spread[:, channels : 2 * channels] = line.astype(jnp.bfloat16)
    spread[:, 2 * channels :] = after.astype(jnp.bfloat16)


def affine_kernel(which, entries, sums, table, *refs):
    film, out = (None, *refs)[-2:]
    channels = table.shape[1]
    center, variance = unpacked_moments(sums[...], entries, channels)
    factor = lax.rsqrt(variance + eps) * table[GAIN + which : GAIN + which + 1]
    offset = table[BIAS + which : BIAS + which + 1]
    if film is not None:
        scale = 1.0 + film[:, :channels]
        factor = factor * scale
        offset = offset * scale + film[:, channels:]
    out[0:1, :] = center
    out[1:2, :] = factor
    out[2:3, :] = offset


def affine(which, cells, sums, table, *film):
    channels = table.shape[1]
    entries = sums.shape[0] * cells * (channels // GROUPS)
    return pl.pallas_call(
        functools.partial(affine_kernel, which, entries),
        out_shape=jax.ShapeDtypeStruct((3, channels), jnp.float32),
        cost_estimate=pl.CostEstimate(flops=0, bytes_accessed=SHADOW_BYTES, transcendentals=0),
        compiler_params=pltpu.CompilerParams(vmem_limit_bytes=VMEM_BYTES),
    )(sums, table, *film)


def tap_copies(source, target, sems):
    return [pltpu.make_async_copy(source.at[tap], target.at[tap], sems.at[tap]) for tap in range(3)]


def convolved(patches, weight, copies):
    total = None
    for tap, copy in enumerate(copies):
        copy.wait()
        part = jnp.dot(patches(tap), weight[tap], preferred_element_type=jnp.float32)
        total = part if total is None else total + part
    return total


def first_kernel(height, breadth, outer, own, norm, table, taps, mate, other, *refs):
    refs = list(refs)
    if outer:
        refs.pop(0)
    result = refs.pop(0)
    packed = None if outer else refs.pop(0)
    weight, spread, sems = refs
    count = lax.axis_size("lat")
    place = lax.axis_index("lat")
    odd = place % 2 == 1
    channels = own.shape[1]
    copies = tap_copies(taps, weight, sems)
    copies[0].start()
    center, factor, offset = norm[0:1, :], norm[1:2, :], norm[2:3, :]
    if outer:
        needed = [-2, -1, 0, height - 1, height, height + 1]
    else:
        needed = list(range(-1, height + 1))
    for i, row in enumerate(needed):
        if row < 0:
            span = slice((row + height) * breadth, (row + height + 1) * breadth)
            values = jnp.where(odd, mate[span, :], other[span, :])
        elif row < height:
            values = own[row * breadth : (row + 1) * breadth, :]
        else:
            span = slice((row - height) * breadth, (row - height + 1) * breadth)
            values = jnp.where(odd, other[span, :], mate[span, :])
        values = silu((values.astype(jnp.float32) - center) * factor + offset)
        if row < 0:
            values = jnp.where(place > 0, values, 0.0)
        elif row >= height:
            values = jnp.where(place < count - 1, values, 0.0)
        shifted(values, spread.at[i * breadth : (i + 1) * breadth, :])
        if i in (1, 3):
            copies[(i + 1) // 2].start()

    def patches(tap):
        if outer:
            pair = [spread[(tap + at) * breadth : (tap + at + 1) * breadth, :] for at in (0, 3)]
            return jnp.concatenate(pair, axis=0)
        return spread[tap * breadth : (tap + height) * breadth, :]

    result[...] = convolved(patches, weight, copies) + table[CONV_BIAS : CONV_BIAS + 1]
    if not outer:
        total, squares = column_sums(result[...])
        packed[...] = jnp.broadcast_to(packed_moments(total, squares), packed.shape)


def first_convolution(height, breadth, own, norm, table, weight, mate, other, after=()):
    channels = own.shape[1]
    count = lax.axis_size("lat")
    outer = len(after) > 0
    rows, needed = (2, 6) if outer else (height, height + 2)
    shape = jax.ShapeDtypeStruct((rows * breadth, channels), jnp.float32)
    return pl.pallas_call(
        functools.partial(first_kernel, height, breadth, outer),
        in_specs=[NEAR] * 3 + [FAR] + [NEAR] * 2 + [FAR] * len(after),
        out_shape=shape if outer else (shape, jax.ShapeDtypeStruct((count, LANES), jnp.float32)),
        scratch_shapes=[
            pltpu.VMEM((3, 3 * channels, channels), jnp.bfloat16),
            pltpu.VMEM((needed * breadth, 3 * channels), jnp.bfloat16),
            pltpu.SemaphoreType.DMA((3,)),
        ],
        compiler_params=pltpu.CompilerParams(vmem_limit_bytes=OUTER_BYTES if outer else VMEM_BYTES),
    )(own, norm, table, weight.reshape(3, 3 * channels, channels), mate, other, *after)


def second_kernel(
    height, breadth, first, outer, own, norm, table, taps, pooled, sent, weight, spread, pairs, sems
):
    count = lax.axis_size("lat")
    place = lax.axis_index("lat")
    channels = own.shape[1]
    weights = tap_copies(taps, weight, sems)
    weights[0].start()
    center, factor, offset = norm[0:1, :], norm[1:2, :], norm[2:3, :]
    for row in [*range(1, height + 1), 0, height + 1]:
        if 0 < row <= height:
            values = first[(row - 1) * breadth : row * breadth, :]
        else:
            at = 0 if row == 0 else breadth
            values = outer[at : at + breadth, :]
        values = silu((values - center) * factor + offset)
        if row == 0:
            values = jnp.where(place > 0, values, 0.0)
        elif row == height + 1:
            values = jnp.where(place < count - 1, values, 0.0)
        shifted(values, spread.at[row * breadth : (row + 1) * breadth, :])
        if row in (2, height + 1):
            weights[1 if row == 2 else 2].start()
    result = convolved(
        lambda tap: spread[tap * breadth : (tap + height) * breadth, :], weight, weights
    )
    level = own[...].astype(jnp.float32) + result + table[CONV_BIAS + 1 : CONV_BIAS + 2]
    level = (level * skip_gain).astype(jnp.bfloat16).astype(jnp.float32)
    half = breadth // 2
    for row in range(height // 2):
        start = 2 * row * breadth
        both = level[start : start + breadth] + level[start + breadth : start + 2 * breadth]
        for tile in range(channels // LANES):
            lanes = slice(tile * LANES, (tile + 1) * LANES)
            pairs[...] = both[:, lanes]
            mean = (pairs[pl.ds(0, half, stride=2), :] + pairs[pl.ds(1, half, stride=2), :]) * 0.25
            pooled[row * half : (row + 1) * half, lanes] = mean
            sent[row * half : (row + 1) * half, lanes] = mean.astype(jnp.bfloat16)


def second_convolution(height, breadth, first, outer, own, norm, table, weight):
    channels = own.shape[1]
    tokens = (height // 2) * (breadth // 2)
    return pl.pallas_call(
        functools.partial(second_kernel, height, breadth),
        in_specs=[NEAR] * 5 + [FAR],
        out_shape=(
            jax.ShapeDtypeStruct((tokens, channels), jnp.float32),
            jax.ShapeDtypeStruct((tokens, channels), jnp.bfloat16),
        ),
        scratch_shapes=[
            pltpu.VMEM((3, 3 * channels, channels), jnp.bfloat16),
            pltpu.VMEM(((height + 2) * breadth, 3 * channels), jnp.bfloat16),
            pltpu.VMEM((breadth, LANES), jnp.float32),
            pltpu.SemaphoreType.DMA((3,)),
        ],
        compiler_params=pltpu.CompilerParams(vmem_limit_bytes=SECOND_BYTES),
    )(first, outer, own, norm, table, weight.reshape(3, 3 * channels, channels))


def exchange(block, stride):
    count = lax.axis_size("lat")
    return lax.ppermute(block, "lat", [(i, i ^ stride) for i in range(count)])


def gather_blocks(block):
    count = lax.axis_size("lat")
    slow = [block] + [exchange(block, stride) for stride in range(4, count, 4)]
    wide = slow + [exchange(each, 2) for each in slow]
    return wide + [exchange(each, 1) for each in wide]


def attention_kernel(count, *refs):
    blocks = refs[:count]
    pooled, table, qkv_weight, proj_weight, out, normed, projected = refs[count:]
    tokens, channels = pooled.shape
    sums, squares = 0.0, 0.0
    for block in blocks:
        more = column_sums(block[...].astype(jnp.float32))
        sums, squares = sums + more[0], squares + more[1]
    row = lax.broadcasted_iota(jnp.int32, (8, channels), 0)
    entries = count * tokens * (channels // GROUPS)
    moments = group_total(jnp.where(row == 0, sums, squares)) / entries
    center = moments[0:1]
    factor = lax.rsqrt(moments[1:2] - center * center + eps) * table[GAIN + 2 : GAIN + 3]
    offset = table[BIAS + 2 : BIAS + 3]

    def norm(values):
        return ((values.astype(jnp.float32) - center) * factor + offset).astype(jnp.bfloat16)

    for i, block in enumerate(blocks):
        normed[i * tokens : (i + 1) * tokens, :] = norm(block[...])
    projected[...] = jnp.dot(
        normed[...], qkv_weight[:, channels:], preferred_element_type=jnp.float32
    ).astype(jnp.bfloat16)
    queries = jnp.dot(
        norm(pooled[...]), qkv_weight[:, :channels], preferred_element_type=jnp.float32
    ).astype(jnp.bfloat16) * jnp.bfloat16(HEAD_DIM ** (-0.5))
    first = lax.broadcasted_iota(jnp.int32, (tokens, 2 * HEAD_DIM), 1) < HEAD_DIM
    starts = range(0, channels, 2 * HEAD_DIM)

    def scored(start):
        query = queries[:, start : start + 2 * HEAD_DIM]
        zero = jnp.zeros_like(query)
        both = jnp.concatenate([jnp.where(first, query, zero), jnp.where(first, zero, query)], axis=0)
        keys = projected[:, start : start + 2 * HEAD_DIM]
        return lax.dot_general(both, keys, (((1,), (1,)), ((), ())), preferred_element_type=jnp.float32)

    attended = []
    later = scored(0)
    for start in starts:
        scores = later
        if start + 2 * HEAD_DIM < channels:
            later = scored(start + 2 * HEAD_DIM)
        weights = jnp.exp(scores - jnp.max(scores, axis=1, keepdims=True))
        totals = jnp.sum(weights, axis=1, keepdims=True)
        values = projected[:, channels + start : channels + start + 2 * HEAD_DIM]
        blended = jnp.dot(weights.astype(jnp.bfloat16), values, preferred_element_type=jnp.float32) / totals
        attended.append(jnp.where(first, blended[:tokens], blended[tokens:]).astype(jnp.bfloat16))
    result = jnp.dot(jnp.concatenate(attended, axis=1), proj_weight[...], preferred_element_type=jnp.float32)
    result = pooled[...] + result + table[PROJ_BIAS : PROJ_BIAS + 1]
    out[...] = (result * skip_gain).astype(jnp.bfloat16)


def attention(blocks, pooled, table, qkv_weight, proj_weight):
    tokens, channels = pooled.shape
    count = len(blocks)
    return pl.pallas_call(
        functools.partial(attention_kernel, count),
        out_shape=jax.ShapeDtypeStruct((tokens, channels), jnp.bfloat16),
        scratch_shapes=[
            pltpu.VMEM((count * tokens, channels), jnp.bfloat16),
            pltpu.VMEM((count * tokens, 2 * channels), jnp.bfloat16),
        ],
        compiler_params=pltpu.CompilerParams(vmem_limit_bytes=(12 + count) * 1024 * 1024),
    )(*blocks, pooled, table, qkv_weight, proj_weight)


def local(
    features,
    noise_index,
    sigma_table,
    affine_weight,
    norm_gain,
    norm_bias,
    conv1_weight,
    conv2_weight,
    conv_bias,
    qkv_weight,
    proj_weight,
    proj_bias,
):
    members, height, breadth, channels = features.shape
    count = lax.axis_size("lat")
    table = jnp.concatenate([norm_gain, norm_bias, conv_bias, proj_bias[None]], axis=0)
    cells = features.reshape(height * breadth, channels)
    packed, own = moments(cells)
    mate = lax.ppermute(cells, "lat", [(i, i ^ 1) for i in range(count)])
    other = lax.ppermute(cells, "lat", [(i, (i - 1 ^ 1) + 1) for i in range(1, count - 1)])
    norm = affine(0, height * breadth, shared(packed), table)
    known = (own, norm, table, conv1_weight, mate, other)
    first, packed = first_convolution(height, breadth, *known)
    outer = first_convolution(height, breadth, *known, [packed])
    film = film_terms(noise_index, sigma_table, affine_weight, packed)
    norm = affine(1, height * breadth, shared(packed), table, film)
    pooled, sent = second_convolution(
        height, breadth, first, outer, cells, norm, table, conv2_weight
    )
    out = attention(gather_blocks(sent), pooled, table, qkv_weight, proj_weight)
    return out.reshape(members, height // 2, breadth // 2, channels)


def solution(mesh):
    return jax.shard_map(
        local,
        mesh=mesh,
        in_specs=(
            P("grp", "lat", None, None),
            P("grp"),
            P(),
            P(),
            P(),
            P(),
            P(),
            P(),
            P(),
            P(),
            P(),
            P(),
        ),
        out_specs=P("grp", "lat", None, None),
        check_vma=False,
    )
```

```python
import functools
import math

import jax
import jax.numpy as jnp
from jax import lax
from jax.experimental import pallas as pl
from jax.experimental.pallas import tpu as pltpu
from jax.sharding import PartitionSpec as P

HEAD_DIM = 64
GROUPS = 32
FREQS = 64
GROUP_WIDTH = 16
LANES = 128
GAIN, BIAS, CONV_BIAS, PROJ_BIAS = 0, 3, 6, 8
VMEM_BYTES = 52 * 1024 * 1024
OUTER_BYTES = 52 * 1024 * 1024
SECOND_BYTES = 51 * 1024 * 1024
FAR = pl.BlockSpec(memory_space=pltpu.HBM)
NEAR = pl.BlockSpec(memory_space=pltpu.VMEM)


eps = 1e-05
skip_gain = 0.7071067811865476


def film_kernel(noise_index, sigma_table, affine_weight, after, out):
    del after
    level = lax.broadcasted_iota(jnp.int32, sigma_table.shape, 1)
    chosen = jnp.where(level == noise_index[0], sigma_table[...], 0.0)
    log_level = jnp.log(jnp.sum(chosen, axis=1, keepdims=True)) / 4.0
    lane = lax.broadcasted_iota(jnp.int32, (1, 2 * FREQS), 1)
    order = (lane % FREQS).astype(jnp.float32)
    angles = log_level * jnp.exp(-math.log(10000.0) * order / FREQS)
    fourier = jnp.where(lane < FREQS, jnp.cos(angles), jnp.sin(angles)).astype(jnp.bfloat16)
    out[...] = jnp.dot(fourier, affine_weight[...], preferred_element_type=jnp.float32)


def film_terms(noise_index, sigma_table, affine_weight, after):
    return pl.pallas_call(
        film_kernel,
        in_specs=[pl.BlockSpec(memory_space=pltpu.SMEM), NEAR, NEAR, FAR],
        out_shape=jax.ShapeDtypeStruct((1, affine_weight.shape[1]), jnp.float32),
        compiler_params=pltpu.CompilerParams(vmem_limit_bytes=VMEM_BYTES),
    )(noise_index, sigma_table[None], affine_weight, after)


def group_total(rows):
    width = rows.shape[1]
    lane = lax.broadcasted_iota(jnp.int32, rows.shape, 1)
    step = 1
    while step < GROUP_WIDTH:
        below = pltpu.roll(rows, step, 1)
        above = pltpu.roll(rows, width - step, 1)
        rows = rows + jnp.where((lane & step) != 0, below, above)
        step *= 2
    return rows


def packed_moments(sums, squares):
    channels = sums.shape[1]
    row = lax.broadcasted_iota(jnp.int32, (8, channels), 0)
    totals = group_total(jnp.where(row == 0, sums, squares))
    slot = lax.broadcasted_iota(jnp.int32, (1, LANES), 1) % GROUP_WIDTH
    packed = jnp.zeros((1, LANES), jnp.float32)
    for tile in range(channels // LANES):
        for kind in range(2):
            part = totals[kind : kind + 1, tile * LANES : (tile + 1) * LANES]
            packed = jnp.where(slot == 2 * tile + kind, part, packed)
    return packed


def unpacked_moments(shared, entries, channels):
    packed = jnp.sum(shared, axis=0, keepdims=True)
    row = lax.broadcasted_iota(jnp.int32, (8, LANES), 0)
    slot = lax.broadcasted_iota(jnp.int32, (8, LANES), 1) % GROUP_WIDTH
    totals = group_total(jnp.where(row == slot, packed, 0.0)) / entries
    tiles = channels // LANES
    center = jnp.concatenate([totals[2 * tile : 2 * tile + 1] for tile in range(tiles)], axis=1)
    second = jnp.concatenate([totals[2 * tile + 1 : 2 * tile + 2] for tile in range(tiles)], axis=1)
    return center, jnp.maximum(second - center * center, 0.0)


def column_sums(values):
    rows, channels = values.shape
    folded = values.reshape(rows // 8, 8, channels)
    sums = jnp.sum(folded, axis=0)
    squares = jnp.sum(folded * folded, axis=0)
    return jnp.sum(sums, axis=0, keepdims=True), jnp.sum(squares, axis=0, keepdims=True)


def silu(values):
    return values / (1.0 + jnp.exp(-values))


def shared(rows):
    count, lanes = rows.shape
    return lax.all_to_all(rows.reshape(count, 1, lanes), "lat", 0, 0).reshape(count, lanes)


def fetched(pairs, sems):
    copies = [pltpu.make_async_copy(source, target, sems.at[i]) for i, (source, target) in enumerate(pairs)]
    for each in copies:
        each.start()
    return copies


def moments_kernel(features, out, held):
    rows = features.shape[0] // 4
    sums, squares = 0.0, 0.0
    for part in range(4):
        values = features[part * rows : (part + 1) * rows, :]
        held[part * rows : (part + 1) * rows, :] = values
        more = column_sums(values.astype(jnp.float32))
        sums, squares = sums + more[0], squares + more[1]
    out[...] = jnp.broadcast_to(packed_moments(sums, squares), out.shape)


def moments(features):
    return pl.pallas_call(
        moments_kernel,
        out_shape=(
            jax.ShapeDtypeStruct((lax.axis_size("lat"), LANES), jnp.float32),
            jax.ShapeDtypeStruct(features.shape, features.dtype),
        ),
        compiler_params=pltpu.CompilerParams(vmem_limit_bytes=VMEM_BYTES),
    )(features)


def shifted(line, spread):
    breadth, channels = line.shape
    column = lax.broadcasted_iota(jnp.int32, line.shape, 0)
    before = jnp.where(column == 0, 0.0, pltpu.roll(line, 1, 0))
    after = jnp.where(column == breadth - 1, 0.0, pltpu.roll(line, breadth - 1, 0))
    spread[:, :channels] = before.astype(jnp.bfloat16)
    spread[:, channels : 2 * channels] = line.astype(jnp.bfloat16)
    spread[:, 2 * channels :] = after.astype(jnp.bfloat16)


def affine_rows(which, cells, sums, table, film=None):
    channels = table.shape[1]
    entries = sums.shape[0] * cells * (channels // GROUPS)
    center, variance = unpacked_moments(sums[...], entries, channels)
    factor = lax.rsqrt(variance + eps) * table[GAIN + which : GAIN + which + 1]
    offset = table[BIAS + which : BIAS + which + 1]
    if film is not None:
        scale = 1.0 + film[:, :channels]
        factor = factor * scale
        offset = offset * scale + film[:, channels:]
    return center, factor, offset


def affine_kernel(which, cells, sums, table, film, out):
    for row, values in enumerate(affine_rows(which, cells, sums, table, film)):
        out[row : row + 1, :] = values


def affine(which, cells, sums, table, film):
    return pl.pallas_call(
        functools.partial(affine_kernel, which, cells),
        out_shape=jax.ShapeDtypeStruct((3, table.shape[1]), jnp.float32),
        compiler_params=pltpu.CompilerParams(vmem_limit_bytes=VMEM_BYTES),
    )(sums, table, film)


def tap_copies(source, target, sems):
    return [pltpu.make_async_copy(source.at[tap], target.at[tap], sems.at[tap]) for tap in range(3)]


def convolved(patches, weight, copies):
    total = None
    for tap, copy in enumerate(copies):
        copy.wait()
        part = jnp.dot(patches(tap), weight[tap], preferred_element_type=jnp.float32)
        total = part if total is None else total + part
    return total


def first_kernel(height, breadth, outer, own, sums, table, taps, mate, other, *refs):
    refs = list(refs)
    if outer:
        refs.pop(0)
    result = refs.pop(0)
    packed = None if outer else refs.pop(0)
    weight, spread, sems = refs
    count = lax.axis_size("lat")
    place = lax.axis_index("lat")
    odd = place % 2 == 1
    channels = own.shape[1]
    copies = tap_copies(taps, weight, sems)
    copies[0].start()
    center, factor, offset = affine_rows(0, height * breadth, sums, table)
    if outer:
        needed = [-2, -1, 0, height - 1, height, height + 1]
    else:
        needed = list(range(-1, height + 1))
    for i, row in enumerate(needed):
        if row < 0:
            span = slice((row + height) * breadth, (row + height + 1) * breadth)
            values = jnp.where(odd, mate[span, :], other[span, :])
        elif row < height:
            values = own[row * breadth : (row + 1) * breadth, :]
        else:
            span = slice((row - height) * breadth, (row - height + 1) * breadth)
            values = jnp.where(odd, other[span, :], mate[span, :])
        values = silu((values.astype(jnp.float32) - center) * factor + offset)
        if row < 0:
            values = jnp.where(place > 0, values, 0.0)
        elif row >= height:
            values = jnp.where(place < count - 1, values, 0.0)
        shifted(values, spread.at[i * breadth : (i + 1) * breadth, :])
        if i in (1, 3):
            copies[(i + 1) // 2].start()

    def patches(tap):
        if outer:
            pair = [spread[(tap + at) * breadth : (tap + at + 1) * breadth, :] for at in (0, 3)]
            return jnp.concatenate(pair, axis=0)
        return spread[tap * breadth : (tap + height) * breadth, :]

    result[...] = convolved(patches, weight, copies) + table[CONV_BIAS : CONV_BIAS + 1]
    if not outer:
        total, squares = column_sums(result[...])
        packed[...] = jnp.broadcast_to(packed_moments(total, squares), packed.shape)


def first_convolution(height, breadth, own, sums, table, weight, mate, other, after=()):
    channels = own.shape[1]
    count = lax.axis_size("lat")
    outer = len(after) > 0
    rows, needed = (2, 6) if outer else (height, height + 2)
    shape = jax.ShapeDtypeStruct((rows * breadth, channels), jnp.float32)
    return pl.pallas_call(
        functools.partial(first_kernel, height, breadth, outer),
        in_specs=[NEAR] * 3 + [FAR] + [NEAR] * 2 + [FAR] * len(after),
        out_shape=shape if outer else (shape, jax.ShapeDtypeStruct((count, LANES), jnp.float32)),
        scratch_shapes=[
            pltpu.VMEM((3, 3 * channels, channels), jnp.bfloat16),
            pltpu.VMEM((needed * breadth, 3 * channels), jnp.bfloat16),
            pltpu.SemaphoreType.DMA((3,)),
        ],
        compiler_params=pltpu.CompilerParams(vmem_limit_bytes=OUTER_BYTES if outer else VMEM_BYTES),
    )(own, sums, table, weight.reshape(3, 3 * channels, channels), mate, other, *after)


def second_kernel(
    height, breadth, first, outer, own, norm, table, taps, pooled, sent, weight, spread, pairs, sems
):
    count = lax.axis_size("lat")
    place = lax.axis_index("lat")
    channels = own.shape[1]
    weights = tap_copies(taps, weight, sems)
    weights[0].start()
    center, factor, offset = norm[0:1, :], norm[1:2, :], norm[2:3, :]
    for row in [*range(1, height + 1), 0, height + 1]:
        if 0 < row <= height:
            values = first[(row - 1) * breadth : row * breadth, :]
        else:
            at = 0 if row == 0 else breadth
            values = outer[at : at + breadth, :]
        values = silu((values - center) * factor + offset)
        if row == 0:
            values = jnp.where(place > 0, values, 0.0)
        elif row == height + 1:
            values = jnp.where(place < count - 1, values, 0.0)
        shifted(values, spread.at[row * breadth : (row + 1) * breadth, :])
        if row in (2, height + 1):
            weights[1 if row == 2 else 2].start()
    result = convolved(
        lambda tap: spread[tap * breadth : (tap + height) * breadth, :], weight, weights
    )
    level = own[...].astype(jnp.float32) + result + table[CONV_BIAS + 1 : CONV_BIAS + 2]
    level = (level * skip_gain).astype(jnp.bfloat16).astype(jnp.float32)
    half = breadth // 2
    for row in range(height // 2):
        start = 2 * row * breadth
        both = level[start : start + breadth] + level[start + breadth : start + 2 * breadth]
        for tile in range(channels // LANES):
            lanes = slice(tile * LANES, (tile + 1) * LANES)
            pairs[...] = both[:, lanes]
            mean = (pairs[pl.ds(0, half, stride=2), :] + pairs[pl.ds(1, half, stride=2), :]) * 0.25
            pooled[row * half : (row + 1) * half, lanes] = mean
            sent[row * half : (row + 1) * half, lanes] = mean.astype(jnp.bfloat16)


def second_convolution(height, breadth, first, outer, own, norm, table, weight):
    channels = own.shape[1]
    tokens = (height // 2) * (breadth // 2)
    return pl.pallas_call(
        functools.partial(second_kernel, height, breadth),
        in_specs=[NEAR] * 5 + [FAR],
        out_shape=(
            jax.ShapeDtypeStruct((tokens, channels), jnp.float32),
            jax.ShapeDtypeStruct((tokens, channels), jnp.bfloat16),
        ),
        scratch_shapes=[
            pltpu.VMEM((3, 3 * channels, channels), jnp.bfloat16),
            pltpu.VMEM(((height + 2) * breadth, 3 * channels), jnp.bfloat16),
            pltpu.VMEM((breadth, LANES), jnp.float32),
            pltpu.SemaphoreType.DMA((3,)),
        ],
        compiler_params=pltpu.CompilerParams(vmem_limit_bytes=SECOND_BYTES),
    )(first, outer, own, norm, table, weight.reshape(3, 3 * channels, channels))


def exchange(block, stride):
    count = lax.axis_size("lat")
    return lax.ppermute(block, "lat", [(i, i ^ stride) for i in range(count)])


def gather_blocks(block):
    count = lax.axis_size("lat")
    slow = [block] + [exchange(block, stride) for stride in range(4, count, 4)]
    wide = slow + [exchange(each, 2) for each in slow]
    return wide + [exchange(each, 1) for each in wide]


def attention_kernel(count, *refs):
    blocks = refs[:count]
    pooled, table, qkv_weight, proj_weight, out, normed, projected = refs[count:]
    tokens, channels = pooled.shape
    sums, squares = 0.0, 0.0
    for block in blocks:
        more = column_sums(block[...].astype(jnp.float32))
        sums, squares = sums + more[0], squares + more[1]
    row = lax.broadcasted_iota(jnp.int32, (8, channels), 0)
    entries = count * tokens * (channels // GROUPS)
    moments = group_total(jnp.where(row == 0, sums, squares)) / entries
    center = moments[0:1]
    variance = jnp.maximum(moments[1:2] - center * center, 0.0)
    factor = lax.rsqrt(variance + eps) * table[GAIN + 2 : GAIN + 3]
    offset = table[BIAS + 2 : BIAS + 3]

    def norm(values):
        return ((values.astype(jnp.float32) - center) * factor + offset).astype(jnp.bfloat16)

    for i, block in enumerate(blocks):
        normed[i * tokens : (i + 1) * tokens, :] = norm(block[...])
    projected[...] = jnp.dot(
        normed[...], qkv_weight[:, channels:], preferred_element_type=jnp.float32
    ).astype(jnp.bfloat16)
    queries = jnp.dot(
        norm(pooled[...]), qkv_weight[:, :channels], preferred_element_type=jnp.float32
    ).astype(jnp.bfloat16) * jnp.bfloat16(HEAD_DIM ** (-0.5))
    first = lax.broadcasted_iota(jnp.int32, (tokens, 2 * HEAD_DIM), 1) < HEAD_DIM
    starts = range(0, channels, 2 * HEAD_DIM)

    def scored(start):
        query = queries[:, start : start + 2 * HEAD_DIM]
        zero = jnp.zeros_like(query)
        both = jnp.concatenate([jnp.where(first, query, zero), jnp.where(first, zero, query)], axis=0)
        keys = projected[:, start : start + 2 * HEAD_DIM]
        return lax.dot_general(both, keys, (((1,), (1,)), ((), ())), preferred_element_type=jnp.float32)

    attended = []
    later = scored(0)
    for start in starts:
        scores = later
        if start + 2 * HEAD_DIM < channels:
            later = scored(start + 2 * HEAD_DIM)
        weights = jnp.exp(scores - jnp.max(scores, axis=1, keepdims=True)).astype(jnp.bfloat16)
        values = projected[:, channels + start : channels + start + 2 * HEAD_DIM]
        values = jnp.concatenate([values, jnp.ones_like(values)], axis=1)
        blended = jnp.dot(weights, values, preferred_element_type=jnp.float32)
        blended = blended[:, : 2 * HEAD_DIM] / blended[:, 2 * HEAD_DIM :]
        attended.append(jnp.where(first, blended[:tokens], blended[tokens:]).astype(jnp.bfloat16))
    result = jnp.dot(jnp.concatenate(attended, axis=1), proj_weight[...], preferred_element_type=jnp.float32)
    result = pooled[...] + result + table[PROJ_BIAS : PROJ_BIAS + 1]
    out[...] = (result * skip_gain).astype(jnp.bfloat16)


def attention(blocks, pooled, table, qkv_weight, proj_weight):
    tokens, channels = pooled.shape
    count = len(blocks)
    return pl.pallas_call(
        functools.partial(attention_kernel, count),
        out_shape=jax.ShapeDtypeStruct((tokens, channels), jnp.bfloat16),
        scratch_shapes=[
            pltpu.VMEM((count * tokens, channels), jnp.bfloat16),
            pltpu.VMEM((count * tokens, 2 * channels), jnp.bfloat16),
        ],
        compiler_params=pltpu.CompilerParams(vmem_limit_bytes=(12 + count) * 1024 * 1024),
    )(*blocks, pooled, table, qkv_weight, proj_weight)


def local(
    features,
    noise_index,
    sigma_table,
    affine_weight,
    norm_gain,
    norm_bias,
    conv1_weight,
    conv2_weight,
    conv_bias,
    qkv_weight,
    proj_weight,
    proj_bias,
):
    members, height, breadth, channels = features.shape
    count = lax.axis_size("lat")
    table = jnp.concatenate([norm_gain, norm_bias, conv_bias, proj_bias[None]], axis=0)
    cells = features.reshape(height * breadth, channels)
    packed, own = moments(cells)
    mate = lax.ppermute(cells, "lat", [(i, i ^ 1) for i in range(count)])
    other = lax.ppermute(cells, "lat", [(i, (i - 1 ^ 1) + 1) for i in range(1, count - 1)])
    sums = shared(packed)
    known = (own, sums, table, conv1_weight, mate, other)
    first, packed = first_convolution(height, breadth, *known)
    outer = first_convolution(height, breadth, *known, [packed])
    film = film_terms(noise_index, sigma_table, affine_weight, packed)
    norm = affine(1, height * breadth, shared(packed), table, film)
    pooled, sent = second_convolution(
        height, breadth, first, outer, cells, norm, table, conv2_weight
    )
    out = attention(gather_blocks(sent), pooled, table, qkv_weight, proj_weight)
    return out.reshape(members, height // 2, breadth // 2, channels)


def solution(mesh):
    return jax.shard_map(
        local,
        mesh=mesh,
        in_specs=(
            P("grp", "lat", None, None),
            P("grp"),
            P(),
            P(),
            P(),
            P(),
            P(),
            P(),
            P(),
            P(),
            P(),
            P(),
        ),
        out_specs=P("grp", "lat", None, None),
        check_vma=False,
    )
```

```python
import functools
import math

import jax
import jax.numpy as jnp
from jax import lax
from jax.experimental import pallas as pl
from jax.experimental.pallas import tpu as pltpu
from jax.sharding import PartitionSpec as P

HEAD_DIM = 64
GROUPS = 32
FREQS = 64
GROUP_WIDTH = 16
LANES = 128
GAIN, BIAS, CONV_BIAS, PROJ_BIAS = 0, 3, 6, 8
VMEM_BYTES = 51 * 1024 * 1024
OUTER_BYTES = 51 * 1024 * 1024
SECOND_BYTES = 51 * 1024 * 1024
FAR = pl.BlockSpec(memory_space=pltpu.HBM)
NEAR = pl.BlockSpec(memory_space=pltpu.VMEM)


eps = 1e-05
skip_gain = 0.7071067811865476


def film_kernel(noise_index, sigma_table, affine_weight, after, out):
    del after
    level = lax.broadcasted_iota(jnp.int32, sigma_table.shape, 1)
    chosen = jnp.where(level == noise_index[0], sigma_table[...], 0.0)
    log_level = jnp.log(jnp.sum(chosen, axis=1, keepdims=True)) / 4.0
    lane = lax.broadcasted_iota(jnp.int32, (1, 2 * FREQS), 1)
    order = (lane % FREQS).astype(jnp.float32)
    angles = log_level * jnp.exp(-math.log(10000.0) * order / FREQS)
    fourier = jnp.where(lane < FREQS, jnp.cos(angles), jnp.sin(angles)).astype(jnp.bfloat16)
    out[...] = jnp.dot(fourier, affine_weight[...], preferred_element_type=jnp.float32)


def film_terms(noise_index, sigma_table, affine_weight, after):
    return pl.pallas_call(
        film_kernel,
        in_specs=[pl.BlockSpec(memory_space=pltpu.SMEM), NEAR, NEAR, FAR],
        out_shape=jax.ShapeDtypeStruct((1, affine_weight.shape[1]), jnp.float32),
        compiler_params=pltpu.CompilerParams(vmem_limit_bytes=VMEM_BYTES),
    )(noise_index, sigma_table[None], affine_weight, after)


def group_total(rows):
    width = rows.shape[1]
    lane = lax.broadcasted_iota(jnp.int32, rows.shape, 1)
    step = 1
    while step < GROUP_WIDTH:
        below = pltpu.roll(rows, step, 1)
        above = pltpu.roll(rows, width - step, 1)
        rows = rows + jnp.where((lane & step) != 0, below, above)
        step *= 2
    return rows


def packed_moments(sums, squares):
    channels = sums.shape[1]
    row = lax.broadcasted_iota(jnp.int32, (8, channels), 0)
    totals = group_total(jnp.where(row == 0, sums, squares))
    slot = lax.broadcasted_iota(jnp.int32, (1, LANES), 1) % GROUP_WIDTH
    packed = jnp.zeros((1, LANES), jnp.float32)
    for tile in range(channels // LANES):
        for kind in range(2):
            part = totals[kind : kind + 1, tile * LANES : (tile + 1) * LANES]
            packed = jnp.where(slot == 2 * tile + kind, part, packed)
    return packed


def unpacked_moments(shared, entries, channels):
    packed = jnp.sum(shared, axis=0, keepdims=True)
    row = lax.broadcasted_iota(jnp.int32, (8, LANES), 0)
    slot = lax.broadcasted_iota(jnp.int32, (8, LANES), 1) % GROUP_WIDTH
    totals = group_total(jnp.where(row == slot, packed, 0.0)) / entries
    tiles = channels // LANES
    center = jnp.concatenate([totals[2 * tile : 2 * tile + 1] for tile in range(tiles)], axis=1)
    second = jnp.concatenate([totals[2 * tile + 1 : 2 * tile + 2] for tile in range(tiles)], axis=1)
    return center, jnp.maximum(second - center * center, 0.0)


def column_sums(values):
    rows, channels = values.shape
    folded = values.reshape(rows // 8, 8, channels)
    sums = jnp.sum(folded, axis=0)
    squares = jnp.sum(folded * folded, axis=0)
    return jnp.sum(sums, axis=0, keepdims=True), jnp.sum(squares, axis=0, keepdims=True)


def silu(values):
    return values / (1.0 + jnp.exp(-values))


def shared(rows):
    count, lanes = rows.shape
    return lax.all_to_all(rows.reshape(count, 1, lanes), "lat", 0, 0).reshape(count, lanes)


def fetched(pairs, sems):
    copies = [pltpu.make_async_copy(source, target, sems.at[i]) for i, (source, target) in enumerate(pairs)]
    for each in copies:
        each.start()
    return copies


def moments_kernel(features, out, held):
    rows = features.shape[0] // 4
    sums, squares = 0.0, 0.0
    for part in range(4):
        values = features[part * rows : (part + 1) * rows, :]
        held[part * rows : (part + 1) * rows, :] = values
        more = column_sums(values.astype(jnp.float32))
        sums, squares = sums + more[0], squares + more[1]
    out[...] = jnp.broadcast_to(packed_moments(sums, squares), out.shape)


def moments(features):
    return pl.pallas_call(
        moments_kernel,
        out_shape=(
            jax.ShapeDtypeStruct((lax.axis_size("lat"), LANES), jnp.float32),
            jax.ShapeDtypeStruct(features.shape, features.dtype),
        ),
        compiler_params=pltpu.CompilerParams(vmem_limit_bytes=VMEM_BYTES),
    )(features)


def shifted(line, spread):
    breadth, channels = line.shape
    column = lax.broadcasted_iota(jnp.int32, line.shape, 0)
    before = jnp.where(column == 0, 0.0, pltpu.roll(line, 1, 0))
    after = jnp.where(column == breadth - 1, 0.0, pltpu.roll(line, breadth - 1, 0))
    spread[:, :channels] = before.astype(jnp.bfloat16)
    spread[:, channels : 2 * channels] = line.astype(jnp.bfloat16)
    spread[:, 2 * channels :] = after.astype(jnp.bfloat16)


def affine_rows(which, cells, sums, table, film=None):
    channels = table.shape[1]
    entries = sums.shape[0] * cells * (channels // GROUPS)
    center, variance = unpacked_moments(sums[...], entries, channels)
    factor = lax.rsqrt(variance + eps) * table[GAIN + which : GAIN + which + 1]
    offset = table[BIAS + which : BIAS + which + 1]
    if film is not None:
        scale = 1.0 + film[:, :channels]
        factor = factor * scale
        offset = offset * scale + film[:, channels:]
    return center, factor, offset


def affine_kernel(which, cells, sums, table, film, out):
    for row, values in enumerate(affine_rows(which, cells, sums, table, film)):
        out[row : row + 1, :] = values


def affine(which, cells, sums, table, film):
    return pl.pallas_call(
        functools.partial(affine_kernel, which, cells),
        out_shape=jax.ShapeDtypeStruct((3, table.shape[1]), jnp.float32),
        compiler_params=pltpu.CompilerParams(vmem_limit_bytes=VMEM_BYTES),
    )(sums, table, film)


def tap_copies(source, target, sems):
    return [pltpu.make_async_copy(source.at[tap], target.at[tap], sems.at[tap]) for tap in range(3)]


def convolved(patches, weight, copies):
    total = None
    for tap, copy in enumerate(copies):
        copy.wait()
        part = jnp.dot(patches(tap), weight[tap], preferred_element_type=jnp.float32)
        total = part if total is None else total + part
    return total


def first_kernel(height, breadth, outer, own, sums, table, taps, mate, other, *refs):
    refs = list(refs)
    if outer:
        refs.pop(0)
    result = refs.pop(0)
    packed = None if outer else refs.pop(0)
    weight, spread, sems = refs
    count = lax.axis_size("lat")
    place = lax.axis_index("lat")
    odd = place % 2 == 1
    channels = own.shape[1]
    copies = tap_copies(taps, weight, sems)
    copies[0].start()
    center, factor, offset = affine_rows(0, height * breadth, sums, table)
    if outer:
        needed = [-2, -1, 0, height - 1, height, height + 1]
    else:
        needed = list(range(-1, height + 1))
    for i, row in enumerate(needed):
        if row < 0:
            span = slice((row + height) * breadth, (row + height + 1) * breadth)
            values = jnp.where(odd, mate[span, :], other[span, :])
        elif row < height:
            values = own[row * breadth : (row + 1) * breadth, :]
        else:
            span = slice((row - height) * breadth, (row - height + 1) * breadth)
            values = jnp.where(odd, other[span, :], mate[span, :])
        values = silu((values.astype(jnp.float32) - center) * factor + offset)
        if row < 0:
            values = jnp.where(place > 0, values, 0.0)
        elif row >= height:
            values = jnp.where(place < count - 1, values, 0.0)
        shifted(values, spread.at[i * breadth : (i + 1) * breadth, :])
        if i in ((2, 4) if outer else (1, 3)):
            copies[i // 2 if outer else (i + 1) // 2].start()

    def patches(tap):
        if outer:
            pair = [spread[(tap + at) * breadth : (tap + at + 1) * breadth, :] for at in (0, 3)]
            return jnp.concatenate(pair, axis=0)
        return spread[tap * breadth : (tap + height) * breadth, :]

    result[...] = convolved(patches, weight, copies) + table[CONV_BIAS : CONV_BIAS + 1]
    if not outer:
        total, squares = column_sums(result[...])
        packed[...] = jnp.broadcast_to(packed_moments(total, squares), packed.shape)


def first_convolution(height, breadth, own, sums, table, weight, mate, other, after=()):
    channels = own.shape[1]
    count = lax.axis_size("lat")
    outer = len(after) > 0
    rows, needed = (2, 6) if outer else (height, height + 2)
    shape = jax.ShapeDtypeStruct((rows * breadth, channels), jnp.float32)
    return pl.pallas_call(
        functools.partial(first_kernel, height, breadth, outer),
        in_specs=[NEAR] * 3 + [FAR] + [NEAR] * 2 + [FAR] * len(after),
        out_shape=shape if outer else (shape, jax.ShapeDtypeStruct((count, LANES), jnp.float32)),
        scratch_shapes=[
            pltpu.VMEM((3, 3 * channels, channels), jnp.bfloat16),
            pltpu.VMEM((needed * breadth, 3 * channels), jnp.bfloat16),
            pltpu.SemaphoreType.DMA((3,)),
        ],
        compiler_params=pltpu.CompilerParams(vmem_limit_bytes=OUTER_BYTES if outer else VMEM_BYTES),
    )(own, sums, table, weight.reshape(3, 3 * channels, channels), mate, other, *after)


def second_kernel(
    height, breadth, first, outer, own, norm, table, taps, pooled, sent, weight, spread, pairs, sems
):
    count = lax.axis_size("lat")
    place = lax.axis_index("lat")
    channels = own.shape[1]
    weights = tap_copies(taps, weight, sems)
    weights[0].start()
    center, factor, offset = norm[0:1, :], norm[1:2, :], norm[2:3, :]
    for row in [*range(1, height + 1), 0, height + 1]:
        if 0 < row <= height:
            values = first[(row - 1) * breadth : row * breadth, :]
        else:
            at = 0 if row == 0 else breadth
            values = outer[at : at + breadth, :]
        values = silu((values - center) * factor + offset)
        if row == 0:
            values = jnp.where(place > 0, values, 0.0)
        elif row == height + 1:
            values = jnp.where(place < count - 1, values, 0.0)
        shifted(values, spread.at[row * breadth : (row + 1) * breadth, :])
        if row in (2, height + 1):
            weights[1 if row == 2 else 2].start()
    result = convolved(
        lambda tap: spread[tap * breadth : (tap + height) * breadth, :], weight, weights
    )
    level = own[...].astype(jnp.float32) + result + table[CONV_BIAS + 1 : CONV_BIAS + 2]
    level = (level * skip_gain).astype(jnp.bfloat16).astype(jnp.float32)
    half = breadth // 2
    for row in range(height // 2):
        start = 2 * row * breadth
        both = level[start : start + breadth] + level[start + breadth : start + 2 * breadth]
        for tile in range(channels // LANES):
            lanes = slice(tile * LANES, (tile + 1) * LANES)
            pairs[...] = both[:, lanes]
            mean = (pairs[pl.ds(0, half, stride=2), :] + pairs[pl.ds(1, half, stride=2), :]) * 0.25
            pooled[row * half : (row + 1) * half, lanes] = mean
            sent[row * half : (row + 1) * half, lanes] = mean.astype(jnp.bfloat16)


def second_convolution(height, breadth, first, outer, own, norm, table, weight):
    channels = own.shape[1]
    tokens = (height // 2) * (breadth // 2)
    return pl.pallas_call(
        functools.partial(second_kernel, height, breadth),
        in_specs=[NEAR] * 5 + [FAR],
        out_shape=(
            jax.ShapeDtypeStruct((tokens, channels), jnp.float32),
            jax.ShapeDtypeStruct((tokens, channels), jnp.bfloat16),
        ),
        scratch_shapes=[
            pltpu.VMEM((3, 3 * channels, channels), jnp.bfloat16),
            pltpu.VMEM(((height + 2) * breadth, 3 * channels), jnp.bfloat16),
            pltpu.VMEM((breadth, LANES), jnp.float32),
            pltpu.SemaphoreType.DMA((3,)),
        ],
        compiler_params=pltpu.CompilerParams(vmem_limit_bytes=SECOND_BYTES),
    )(first, outer, own, norm, table, weight.reshape(3, 3 * channels, channels))


def exchange(block, stride):
    count = lax.axis_size("lat")
    return lax.ppermute(block, "lat", [(i, i ^ stride) for i in range(count)])


def gather_blocks(block):
    count = lax.axis_size("lat")
    slow = [block] + [exchange(block, stride) for stride in range(4, count, 4)]
    wide = slow + [exchange(each, 2) for each in slow]
    return wide + [exchange(each, 1) for each in wide]


def attention_kernel(count, *refs):
    blocks = refs[:count]
    pooled, table, qkv_weight, proj_weight, out, normed, projected = refs[count:]
    tokens, channels = pooled.shape
    sums, squares = 0.0, 0.0
    for block in blocks:
        more = column_sums(block[...].astype(jnp.float32))
        sums, squares = sums + more[0], squares + more[1]
    row = lax.broadcasted_iota(jnp.int32, (8, channels), 0)
    entries = count * tokens * (channels // GROUPS)
    moments = group_total(jnp.where(row == 0, sums, squares)) / entries
    center = moments[0:1]
    variance = jnp.maximum(moments[1:2] - center * center, 0.0)
    factor = lax.rsqrt(variance + eps) * table[GAIN + 2 : GAIN + 3]
    offset = table[BIAS + 2 : BIAS + 3]

    def norm(values):
        return ((values.astype(jnp.float32) - center) * factor + offset).astype(jnp.bfloat16)

    for i, block in enumerate(blocks):
        normed[i * tokens : (i + 1) * tokens, :] = norm(block[...])
    projected[...] = jnp.dot(
        normed[...], qkv_weight[:, channels:], preferred_element_type=jnp.float32
    ).astype(jnp.bfloat16)
    queries = jnp.dot(
        norm(pooled[...]), qkv_weight[:, :channels], preferred_element_type=jnp.float32
    ).astype(jnp.bfloat16) * jnp.bfloat16(HEAD_DIM ** (-0.5))
    first = lax.broadcasted_iota(jnp.int32, (tokens, 2 * HEAD_DIM), 1) < HEAD_DIM
    starts = range(0, channels, 2 * HEAD_DIM)

    def scored(start):
        query = queries[:, start : start + 2 * HEAD_DIM]
        zero = jnp.zeros_like(query)
        both = jnp.concatenate([jnp.where(first, query, zero), jnp.where(first, zero, query)], axis=0)
        keys = projected[:, start : start + 2 * HEAD_DIM]
        return lax.dot_general(both, keys, (((1,), (1,)), ((), ())), preferred_element_type=jnp.float32)

    attended = []
    later = scored(0)
    for start in starts:
        scores = later
        if start + 2 * HEAD_DIM < channels:
            later = scored(start + 2 * HEAD_DIM)
        weights = jnp.exp(scores - jnp.max(scores, axis=1, keepdims=True)).astype(jnp.bfloat16)
        values = projected[:, channels + start : channels + start + 2 * HEAD_DIM]
        values = jnp.concatenate([values, jnp.ones_like(values)], axis=1)
        blended = jnp.dot(weights, values, preferred_element_type=jnp.float32)
        blended = blended[:, : 2 * HEAD_DIM] / blended[:, 2 * HEAD_DIM :]
        attended.append(jnp.where(first, blended[:tokens], blended[tokens:]).astype(jnp.bfloat16))
    result = jnp.dot(jnp.concatenate(attended, axis=1), proj_weight[...], preferred_element_type=jnp.float32)
    result = pooled[...] + result + table[PROJ_BIAS : PROJ_BIAS + 1]
    out[...] = (result * skip_gain).astype(jnp.bfloat16)


def attention(blocks, pooled, table, qkv_weight, proj_weight):
    tokens, channels = pooled.shape
    count = len(blocks)
    return pl.pallas_call(
        functools.partial(attention_kernel, count),
        out_shape=jax.ShapeDtypeStruct((tokens, channels), jnp.bfloat16),
        scratch_shapes=[
            pltpu.VMEM((count * tokens, channels), jnp.bfloat16),
            pltpu.VMEM((count * tokens, 2 * channels), jnp.bfloat16),
        ],
        compiler_params=pltpu.CompilerParams(vmem_limit_bytes=(12 + count) * 1024 * 1024),
    )(*blocks, pooled, table, qkv_weight, proj_weight)


def local(
    features,
    noise_index,
    sigma_table,
    affine_weight,
    norm_gain,
    norm_bias,
    conv1_weight,
    conv2_weight,
    conv_bias,
    qkv_weight,
    proj_weight,
    proj_bias,
):
    members, height, breadth, channels = features.shape
    count = lax.axis_size("lat")
    table = jnp.concatenate([norm_gain, norm_bias, conv_bias, proj_bias[None]], axis=0)
    cells = features.reshape(height * breadth, channels)
    packed, own = moments(cells)
    mate = lax.ppermute(cells, "lat", [(i, i ^ 1) for i in range(count)])
    other = lax.ppermute(cells, "lat", [(i, (i - 1 ^ 1) + 1) for i in range(1, count - 1)])
    sums = shared(packed)
    known = (own, sums, table, conv1_weight, mate, other)
    first, packed = first_convolution(height, breadth, *known)
    outer = first_convolution(height, breadth, *known, [packed])
    film = film_terms(noise_index, sigma_table, affine_weight, packed)
    norm = affine(1, height * breadth, shared(packed), table, film)
    pooled, sent = second_convolution(
        height, breadth, first, outer, cells, norm, table, conv2_weight
    )
    out = attention(gather_blocks(sent), pooled, table, qkv_weight, proj_weight)
    return out.reshape(members, height // 2, breadth // 2, channels)


def solution(mesh):
    return jax.shard_map(
        local,
        mesh=mesh,
        in_specs=(
            P("grp", "lat", None, None),
            P("grp"),
            P(),
            P(),
            P(),
            P(),
            P(),
            P(),
            P(),
            P(),
            P(),
            P(),
        ),
        out_specs=P("grp", "lat", None, None),
        check_vma=False,
    )
```
